32 devices in a mesh: grp: 4 (over y, core), tile: 8 (over z, x).
Axes of the slice: x: 2, y: 2, z: 4, core: 2. Of those that a mesh axis runs over, the one named last changes fastest.
Arguments:
- members: float32 [32, 32, 64, 128], P(None, 'grp', 'tile'), may hold values from -6 to 6
- courant: float32 [3, 32, 64, 128], P(None, 'grp', 'tile'), may hold values from -0.08 to 0.08
- turb_energy: float32 [32, 64, 128], P('grp', 'tile'), may hold values from 0.3 to 1
- dissipation: float32 [32, 64, 128], P('grp', 'tile'), may hold values from 1 to 10
- sensor_cells: int32 [8, 32768], P(None, ('grp', 'tile')), may hold values from 0 to 8191, as said below
- sensor_frac: float32 [3, 32768], P(None, ('grp', 'tile')), may hold values from 0 to 1
- sensor_count: int32 [32], P(('grp', 'tile')), may hold values from 1 to 1024, 16384 in all
- obs_var: float32 [16384], P('tile'), may hold values from 0.2 to 1
Outputs:
- trailing: float32 [16384, 16384], P('grp', 'tile')
- factor: float32 [16384, 512], P(('grp', 'tile'))
The draws below stay inside these ranges and needn't reach their ends.
Inputs may be any that keep to these rules, and one draw needn't show every extreme that they name: `sensor_cells`: slot q lists the eight cells of a cube of 2 x 2 x 2 cells inside its grid block, as local indices (x 8 + y) * 128 + z; entry j is the corner offset by the bits of j (first dimension most significant), entry 0 the lowest corner. `sensor_count`: the counts sum to 16384.
All inputs are finite; a program needn't handle non-finite values. No bound on the sum of `sensor_count` on one device may be relied on, other than what follows from the above.
Results may differ from the reference program's by a relative error of at most 0.0025.
Values sent between devices are 32-bit elements; how exact they have to be, the bound alone decides.
No kernel may reach another device: no remote copies, remote signals or barrier semaphores. Data moves between devices by JAX's collectives and lax.ppermute only.
A program may use at most 192 MiB of HBM per device.

```python
import math
import jax
import jax.numpy as jnp
import numpy as np
from jax import lax

CX = 8
CY = 8
CZ = 128
M = 32
NS = 16384
PANEL = 128
PANELS = 4
SWEEPS = 2
LOC = 8
SENS_MOST = 1024
SLOTS = 32768
NX = 32
NY = 64
N_TILE = 8
DEVICES = 32


def draw_sensor_cells(key, part):
    key = jax.random.fold_in(key, 11)
    key_x, key_y, key_z = jax.random.split(key, 3)
    base_x = jax.random.randint(key_x, (SLOTS,), 0, CX - 1)
    base_y = jax.random.randint(key_y, (SLOTS,), 0, CY - 1)
    base_z = jax.random.randint(key_z, (SLOTS,), 0, CZ - 1)
    corners = []
    for step_x in range(2):
        for step_y in range(2):
            for step_z in range(2):
                corners.append(((base_x + step_x) * CY + base_y + step_y) * CZ + base_z + step_z)
    return jnp.stack(corners, 0).astype(jnp.int32)


def block_levels(own_key, shape, cuts, smallest, top_value):
    gain, own = 1.0, jax.random.fold_in(own_key, 6)
    for axis_at, blocks in cuts:
        heights = jnp.exp(jax.random.uniform(jax.random.fold_in(own, axis_at), (blocks,), jnp.float32, smallest / len(cuts), top_value / len(cuts)))
        gain = gain * jnp.repeat(heights, shape[axis_at] // blocks).reshape([-1 if axis == axis_at else 1 for axis in range(len(shape))])
    return gain


def split_up(number_of, total, limit, slope):
    loads = [(1 << 20) // math.isqrt(grade ** slope) + 1 for grade in range(2, number_of + 1)]
    spare, counts = total - limit - (number_of - 1), [1] * (number_of - 1)
    while spare > 0:
        free = [i for i in range(number_of - 1) if counts[i] < limit]
        whole, remaining = sum([loads[i] for i in free]), spare
        for i in free:
            more = min(limit - counts[i], max(1, remaining * loads[i] // whole), spare)
            counts[i] = counts[i] + more
            spare = spare - more
    return np.array([limit] + counts)


def ragged(own_key, amount, total, bound, skew):
    if amount == 2:
        one = jax.random.randint(own_key, (), max(1, total - bound), min(bound, total - 1) + 1)
        return jnp.stack([one, total - one])
    tallies = jnp.asarray(split_up(amount, total, bound, skew), jnp.int32)
    couples = (amount - 1) // 2
    source_of, receiver = tallies[1:1 + 2 * couples:2], tallies[2:2 + 2 * couples:2]
    room = jnp.minimum(source_of - 1, bound - receiver)
    shifted = jax.random.randint(jax.random.fold_in(own_key, 1), (couples,), 0, 1 << 20) % (room + 1)
    tallies = tallies.at[1:1 + 2 * couples:2].set(source_of - shifted).at[2:2 + 2 * couples:2].set(receiver + shifted)
    return tallies[jax.random.permutation(jax.random.fold_in(own_key, 2), amount)]


def normal_values(rng, shape, deviation, most, shards=(), held_as=jnp.bfloat16):
    drawn = jax.random.normal(rng, shape, jnp.float32) * deviation
    if len(shards) > 0:
        drawn = block_levels(rng, shape, shards, -0.22, 0.18) * drawn
    return jnp.clip(drawn, min=-most, max=most).astype(held_as)


def setup_inputs(seed: int = 0) -> dict:
    key_list = jax.random.split(jax.random.key(seed), 9)
    members = normal_values(key_list[0], (M, NX, NY, CZ), 1.0, 6.0, ((1, 4), (2, 8)), jnp.float32)
    courant = jnp.clip(jax.random.uniform(key_list[1], (3, NX, NY, CZ), jnp.float32, -0.08, 0.08) * block_levels(key_list[1], (3, NX, NY, CZ), ((1, 4), (2, 8)), -0.4, 0.0), -0.08, 0.08)
    turb_energy = jnp.clip(0.3 + 0.7 * jax.random.uniform(key_list[2], (NX, NY, CZ), jnp.float32) ** block_levels(key_list[2], (NX, NY, CZ), ((0, 4), (1, 8)), -0.2, 0.2), 0.3, 1.0)
    dissipation = jnp.clip(jnp.exp(math.log(10.0) - 2.3025851 * jax.random.uniform(key_list[3], (NX, NY, CZ), jnp.float32) ** block_levels(key_list[3], (NX, NY, CZ), ((0, 4), (1, 8)), -0.2, 0.2)), 1.0, 10.0)
    sensor_cells = draw_sensor_cells(jax.random.fold_in(key_list[8], 71), 0)
    sensor_frac = jnp.clip(1.0 * jax.random.uniform(key_list[5], (3, SLOTS), jnp.float32) ** block_levels(key_list[5], (3, SLOTS), ((1, 32),), -0.2, 0.2), 0.0, 1.0)
    sensor_count = ragged(key_list[6], DEVICES, NS, SENS_MOST, 2).astype(jnp.int32)
    obs_var = jnp.clip(jnp.exp(math.log(1.0) - 1.609438 * jax.random.uniform(key_list[7], (NS,), jnp.float32) ** block_levels(key_list[7], (NS,), ((0, 8),), -0.2, 0.2)), 0.2, 1.0)
    return {"members": members, "courant": courant, "turb_energy": turb_energy, "dissipation": dissipation, "sensor_cells": sensor_cells, "sensor_frac": sensor_frac, "sensor_count": sensor_count, "obs_var": obs_var}


diffuse_rate = 0.06

def window(array_in, spatial, lower_cut, upper_cut):
    pieces = []
    for dimension in range(3):
        extent = array_in.shape[array_in.ndim - 3 + dimension]
        if dimension == spatial:
            pieces.append(slice(lower_cut, extent - upper_cut))
        else:
            pieces.append(slice(1, extent - 1))
    return array_in[(slice(None),) * (array_in.ndim - 3) + tuple(pieces)]

def advance(padded, coefs):
    interior = window(padded, 0, 1, 1)
    change = jnp.zeros_like(interior)
    for spatial in range(3):
        lower_cells = window(padded, spatial, 0, 1)
        upper_cells = window(padded, spatial, 1, 0)
        speed_face = 0.5 * (window(coefs[spatial], spatial, 0, 1) + window(coefs[spatial], spatial, 1, 0))
        spread_face = 0.5 * (window(coefs[3], spatial, 0, 1) + window(coefs[3], spatial, 1, 0))
        flux_face = jnp.maximum(speed_face, 0.0) * lower_cells + jnp.minimum(speed_face, 0.0) * upper_cells + spread_face * (lower_cells - upper_cells)
        dimension = flux_face.ndim - 3 + spatial
        extent = flux_face.shape[dimension]
        change = change + lax.slice_in_dim(flux_face, 1, extent, axis=dimension) - lax.slice_in_dim(flux_face, 0, extent - 1, axis=dimension)
    return interior - change

def corner_weights(fractions):
    rows_out = []
    for corner in range(8):
        weight_now = jnp.ones_like(fractions[0])
        for spatial in range(3):
            if corner >> 2 - spatial & 1:
                weight_now = weight_now * fractions[spatial]
            else:
                weight_now = weight_now * (1.0 - fractions[spatial])
        rows_out.append(weight_now)
    return jnp.stack(rows_out, 0)

def reference(members, courant, turb_energy, dissipation, sensor_cells, sensor_frac, sensor_count, obs_var):
    diffusion = diffuse_rate * turb_energy * turb_energy / dissipation
    coefs = jnp.pad(jnp.concatenate([courant, diffusion[None]], 0), ((0, 0), (1, 1), (1, 1), (1, 1)))
    state = members
    for sweep_index in range(SWEEPS):
        state = advance(jnp.pad(state, ((0, 0), (1, 1), (1, 1), (1, 1))), coefs)
    anomaly = state - jnp.mean(state, axis=0, keepdims=True)
    slot_ids = jnp.arange(SLOTS, dtype=jnp.int32)
    block_id = slot_ids // SENS_MOST
    block_x = block_id // N_TILE
    block_y = block_id % N_TILE
    local_x = sensor_cells // (CY * CZ)
    local_y = sensor_cells // CZ % CY
    local_z = sensor_cells % CZ
    global_x = block_x[None, :] * CX + local_x
    global_y = block_y[None, :] * CY + local_y
    flat_index = ((global_x * NY + global_y) * CZ + local_z).astype(jnp.int32)
    picked = jnp.take(anomaly.reshape(M, -1), flat_index, axis=1)
    weights = corner_weights(sensor_frac)
    response = jnp.sum(picked * weights[None], axis=1).astype(jnp.bfloat16)
    position = jnp.stack([global_x[0].astype(jnp.float32) + sensor_frac[0], global_y[0].astype(jnp.float32) + sensor_frac[1], local_z[0].astype(jnp.float32) + sensor_frac[2]], 0)
    offsets = (jnp.cumsum(sensor_count) - sensor_count).astype(jnp.int32)
    local_slot = slot_ids % SENS_MOST
    packed = jnp.where(local_slot < sensor_count[block_id], offsets[block_id] + local_slot, NS).astype(jnp.int32)
    packed_response = jnp.zeros((M, NS), jnp.bfloat16).at[:, packed].set(response, mode='drop')
    packed_position = jnp.zeros((3, NS), jnp.float32).at[:, packed].set(position, mode='drop')
    covar = jnp.dot(packed_response.T.astype(jnp.float32), packed_response.astype(jnp.float32), preferred_element_type=jnp.float32)
    dist_sq = jnp.zeros((NS, NS), jnp.float32)
    for spatial in range(3):
        gap_now = packed_position[spatial][:, None] - packed_position[spatial][None, :]
        dist_sq = dist_sq + gap_now * gap_now
    taper = 1.0 / (1.0 + dist_sq / (LOC * LOC))
    matrix = taper * covar / (M - 1)
    diag_ids = jnp.arange(NS, dtype=jnp.int32)
    matrix = matrix.at[diag_ids, diag_ids].add(obs_var)
    columns_out = []
    for panel_index in range(PANELS):
        start = panel_index * PANEL
        lower_block = jnp.linalg.cholesky(matrix[start:start + PANEL, start:start + PANEL])
        column_block = lax.linalg.triangular_solve(lower_block, matrix[:, start:start + PANEL], left_side=False, lower=True, transpose_a=True)
        column_block = jnp.where((diag_ids >= start)[:, None], column_block, 0.0)
        matrix = matrix - jnp.dot(column_block.astype(jnp.float32), column_block.T.astype(jnp.float32), preferred_element_type=jnp.float32, precision=lax.Precision.HIGHEST)
        columns_out.append(column_block)
    return (matrix, jnp.concatenate(columns_out, 1))
```

```python
import jax
import jax.numpy as jnp
from jax import lax
from jax.experimental import pallas as pl
from jax.experimental.pallas import tpu as pltpu
from jax.sharding import PartitionSpec as P

NS = 16384
PANEL = 128
PANELS = 4
SWEEPS = 2
LOC = 8
HEAD = PANEL * PANELS
ROWS = 40
LANES = 128

diffuse_rate = 0.06

HIGH = lax.Precision.HIGHEST
F32 = jnp.float32
BF16 = jnp.bfloat16
VMEM_LIMIT = 56 * 1024 * 1024


def split(value):
    hi = value.astype(BF16)
    lo = (value - hi.astype(F32)).astype(BF16)
    return hi, lo


def forecast_kernel(
    place_ref, count_ref, mem, cour, turb, diss, xlo, xhi, ylo, yhi, own_lo, own_hi,
    c_ll, c_lh, c_hl, c_hh, cells, frac, obs, out, kc, state,
):
    members_n = mem.shape[0]
    slots = cells.shape[1]
    grp, tile = place_ref[0], place_ref[1]
    last_grp, last_tile = place_ref[2], place_ref[3]
    sub = lax.broadcasted_iota(jnp.int32, (8, LANES), 0)
    lane = lax.broadcasted_iota(jnp.int32, (8, LANES), 1)

    def after(v, row):
        return jnp.where(sub == 0, jnp.broadcast_to(row, (8, LANES)), pltpu.roll(v, 1, 0))

    def before(v, row):
        return jnp.where(sub == 7, jnp.broadcast_to(row, (8, LANES)), pltpu.roll(v, 7, 0))

    def zlow(v):
        return jnp.where(lane == 0, 0.0, pltpu.roll(v, 1, 1))

    def zhigh(v):
        return jnp.where(lane == LANES - 1, 0.0, pltpu.roll(v, LANES - 1, 1))

    def diffusion(x):
        t = turb[x]
        return diffuse_rate * t * t / diss[x]

    def xplane(f, x):
        if x < 0:
            return xlo[f, x + 2]
        if x > 7:
            return xhi[f, x - 8]
        if isinstance(f, int) and f >= members_n:
            return cour[f - members_n, x] if f < members_n + 3 else diffusion(x)
        return mem[f, x]

    def row(ref, f):
        return ref[pl.ds(f, 1), :]

    def xends(f, x):
        if x < 0:
            return row(c_ll, f), row(c_lh, f)
        if x > 7:
            return row(c_hl, f), row(c_hh, f)
        return ylo[f, 1, x : x + 1, :], yhi[f, 0, x : x + 1, :]

    def face(cp, ep, cq, eq):
        c = 0.5 * (cp + cq)
        e = 0.5 * (ep + eq)
        return jnp.maximum(c, 0.0) + e, jnp.minimum(c, 0.0) - e

    def coefs(index, keep, depth, tangent, planes, ends):
        e_prev, e_now, e_next = planes(members_n + 3)
        e_lo, e_hi = ends(members_n + 3)
        d_prev, d_now, d_next = planes(members_n + depth)
        t_now = planes(members_n + tangent)[1]
        t_lo, t_hi = ends(members_n + tangent)
        z_now = planes(members_n + 2)[1]
        pairs = [
            face(d_prev, e_prev, d_now, e_now),
            face(d_now, e_now, d_next, e_next),
            face(after(t_now, t_lo), after(e_now, e_lo), t_now, e_now),
            face(t_now, e_now, before(t_now, t_hi), before(e_now, e_hi)),
            face(zlow(z_now), zlow(e_now), z_now, e_now),
            face(z_now, e_now, zhigh(z_now), zhigh(e_now)),
        ]
        middle = jnp.ones((8, LANES), F32)
        for axis in range(3):
            (a_lo, b_lo), (a_hi, b_hi) = pairs[2 * axis], pairs[2 * axis + 1]
            middle = middle - (a_hi - b_lo)
            kc[index, 1 + 2 * axis] = keep * a_lo
            kc[index, 2 + 2 * axis] = -(keep * b_hi)
        kc[index, 0] = keep * middle

    def kept(flag):
        return jnp.where(flag, 1.0, 0.0).astype(F32)

    for x in range(-1, 9):
        keep = 1.0
        if x < 0:
            keep = kept(grp > 0)
        if x > 7:
            keep = kept(grp < last_grp)
        coefs(
            x + 1, keep, 0, 1,
            lambda f, x=x: tuple(xplane(f, x + s) for s in (-1, 0, 1)),
            lambda f, x=x: xends(f, x),
        )

    def yplanes_lo(f):
        return ylo[f, 0], ylo[f, 1], own_lo[f, 0]

    def yplanes_hi(f):
        return own_hi[f, 1], yhi[f, 0], yhi[f, 1]

    def yends_lo(f):
        return row(c_ll, f), row(c_hl, f)

    def yends_hi(f):
        return row(c_lh, f), row(c_hh, f)

    coefs(10, kept(tile > 0), 1, 0, yplanes_lo, yends_lo)
    coefs(11, kept(tile < last_tile), 1, 0, yplanes_hi, yends_hi)

    def update(index, v_prev, v, v_next, r_lo, r_hi):
        return (
            kc[index, 0] * v
            + kc[index, 1] * v_prev
            + kc[index, 2] * v_next
            + kc[index, 3] * after(v, r_lo)
            + kc[index, 4] * before(v, r_hi)
            + kc[index, 5] * zlow(v)
            + kc[index, 6] * zhigh(v)
        )

    def one_member(m, total):
        planes = [xplane(m, x) for x in range(-2, 10)]
        new = [
            update(x + 1, planes[x + 1], planes[x + 2], planes[x + 3], *xends(m, x))
            for x in range(-1, 9)
        ]
        new_lo = update(10, *yplanes_lo(m), *yends_lo(m))
        new_hi = update(11, *yplanes_hi(m), *yends_hi(m))
        sums = []
        for x in range(8):
            v = update(
                x + 1, new[x], new[x + 1], new[x + 2], new_lo[x : x + 1, :], new_hi[x : x + 1, :]
            )
            state[m, x * 8 : (x + 1) * 8, :] = v
            sums.append(total[x] + v)
        return tuple(sums)

    zero = jnp.zeros((8, LANES), F32)
    total = lax.fori_loop(0, members_n, one_member, (zero,) * 8)
    mean = jnp.concatenate(total, 0) * (1.0 / members_n)

    base = cells[0:1, :]
    z0 = lax.rem(base, LANES)
    xy0 = lax.div(base, LANES)
    y0 = lax.rem(xy0, 8)
    x0 = lax.div(xy0, 8)
    fx, fy, fz = frac[0:1, :], frac[1:2, :], frac[2:3, :]

    def hat(size, at, f):
        iota = lax.broadcasted_iota(jnp.int32, (size, slots), 0)
        return jnp.where(iota == at, 1.0 - f, jnp.where(iota == at + 1, f, 0.0))

    wz_hi, wz_lo = split(hat(LANES, z0, fz))
    wz = jnp.concatenate([wz_hi, wz_hi, wz_lo], 0)
    wx = hat(8, x0, fx)
    wy = hat(8, y0, fy)
    wxy = jnp.concatenate([wx[x : x + 1, :] * wy for x in range(8)], 0)

    group = 8

    def some_members(step, carry):
        field = state[pl.ds(step * group, group)] - mean[None]
        hi, lo = split(field.reshape(group * 64, LANES))
        along = jnp.dot(
            jnp.concatenate([hi, lo, hi], 1), wz, preferred_element_type=F32
        ).reshape(group, 64, slots)
        picked = jnp.sum(along * wxy[None], axis=1)
        out[pl.ds(pl.multiple_of(step * group, group), group), :] = picked.astype(BF16).astype(F32)
        return carry

    lax.fori_loop(0, members_n // group, some_members, 0)
    tail = jnp.concatenate(
        [
            (grp * 8 + x0).astype(F32) + fx,
            (tile * 8 + y0).astype(F32) + fy,
            z0.astype(F32) + fz,
            jnp.full((1, slots), count_ref[0], jnp.int32).astype(F32),
            obs[...],
            jnp.zeros((3, slots), F32),
        ],
        0,
    )
    out[members_n : members_n + 8, :] = tail


def taper_cov(left, right, members_n):
    cov = jnp.dot(
        left[:, :members_n].astype(BF16), right[:members_n].astype(BF16), preferred_element_type=F32
    )
    dist = None
    for d in range(3):
        at = members_n + d
        gap = left[:, at : at + 1] - right[at : at + 1, :]
        dist = gap * gap if dist is None else dist + gap * gap
    scale = 1.0 / (members_n - 1.0)
    return cov * (scale / (1.0 + dist * (1.0 / (LOC * LOC))))


def eliminate(a):
    groups = len(a)
    sub = lax.broadcasted_iota(jnp.int32, (8, LANES), 0)
    lane = lax.broadcasted_iota(jnp.int32, (8, LANES), 1)
    m = [jnp.where(lane == sub + 8 * g, 1.0, 0.0).astype(F32) for g in range(groups)]
    done = []

    def down(v, j):
        return jnp.broadcast_to(v[j : j + 1, :], (8, LANES))

    def across(v, k):
        return jnp.broadcast_to(v[:, k : k + 1], (8, LANES))

    for gk in range(groups):
        k0 = 8 * gk
        col = [across(a[gk], k0 + j) for j in range(8)]
        ra, rm = a[gk], m[gk]
        rows_a, rows_m, inv, u = [], [], [], []
        diag = jnp.ones((8, LANES), F32)
        for j in range(8):
            pivot = down(col[j], j)
            r = 1.0 / pivot
            diag = jnp.where(sub == j, pivot, diag)
            row_a, row_m = down(ra, j), down(rm, j)
            uj = [down(col[i], j) if i > j else None for i in range(8)]
            f = jnp.where(sub > j, col[j] * r, 0.0)
            for i in range(j + 1, 8):
                col[i] = col[i] - f * uj[i]
            ra = ra - f * row_a
            rm = rm - f * row_m
            rows_a.append(row_a)
            rows_m.append(row_m)
            inv.append(r)
            u.append(uj)
        done.append(rm * lax.rsqrt(diag))
        for g in range(gk + 1, groups):
            c = [across(a[g], k0 + j) for j in range(8)]
            ag, mg = a[g], m[g]
            for j in range(8):
                f = c[j] * inv[j]
                for i in range(j + 1, 8):
                    c[i] = c[i] - f * u[j][i]
                ag = ag - f * rows_a[j]
                mg = mg - f * rows_m[j]
            a[g], m[g] = ag, mg
    return jnp.concatenate(done, 0)


def head_kernel(
    offset_ref, place_ref, everything, obs_head, rows_out, cols_out, head_out, linv_out, fcols_out,
    full, work,
):
    blocks, _, slots = everything.shape
    row_chunks = rows_out.shape[0] // LANES
    col_chunks = cols_out.shape[1] // LANES
    members_n = ROWS - 8
    grp, tile = place_ref[0], place_ref[1]
    lane = lax.broadcasted_iota(jnp.int32, (ROWS, LANES), 1)
    parts = slots // LANES

    def pack(b, carry):
        at = offset_ref[b]
        chunk = lax.div(at, LANES)
        shift = lax.rem(at, LANES)
        early = lane < shift
        last = full[chunk]
        for j in range(parts):
            now = pltpu.roll(everything[b, :, j * LANES : (j + 1) * LANES], shift, 1)
            full[chunk + j] = jnp.where(early, last, now)
            last = now
        full[chunk + parts] = last
        return carry

    lax.fori_loop(0, blocks, pack, 0)

    def turn(c, carry):
        piece = jnp.concatenate([full[grp * row_chunks + c], jnp.zeros((LANES - ROWS, LANES), F32)], 0)
        rows_out[pl.ds(pl.multiple_of(c * LANES, LANES), LANES), :] = piece.T
        return carry

    lax.fori_loop(0, row_chunks, turn, 0)
    for c in range(col_chunks):
        cols_out[:, c * LANES : (c + 1) * LANES] = full[tile * col_chunks + c]
    for c in range(PANELS):
        head_out[:, c * LANES : (c + 1) * LANES] = full[c]

    head = head_out[...]
    down = []
    for c in range(PANELS):
        piece = jnp.concatenate([full[c], jnp.zeros((LANES - ROWS, LANES), F32)], 0)
        down.append(piece.T)
    down = jnp.concatenate(down, 0)
    rid = lax.broadcasted_iota(jnp.int32, (HEAD, HEAD), 0)
    cid = lax.broadcasted_iota(jnp.int32, (HEAD, HEAD), 1)
    same = rid == cid
    work[:HEAD, :HEAD] = taper_cov(down, head, members_n) + jnp.where(same, obs_head[...], 0.0)
    work[:HEAD, HEAD:] = jnp.where(same, 1.0, 0.0).astype(F32)

    def panel(p, carry):
        at = pl.multiple_of(p * PANEL, PANEL)
        for q in range(PANELS):
            @pl.when(p == q)
            def _(q=q):
                for g in range(16):
                    work[HEAD + 8 * g : HEAD + 8 * g + 8, :PANEL] = work[
                        q * PANEL + 8 * g : q * PANEL + 8 * g + 8, q * PANEL : (q + 1) * PANEL
                    ]
        inverse = eliminate([work[HEAD + 8 * g : HEAD + 8 * g + 8, :PANEL] for g in range(16)])
        done = jnp.dot(inverse, work[pl.ds(at, PANEL), :], precision=HIGH, preferred_element_type=F32)
        work[pl.ds(at, PANEL), :] = done
        for q in range(PANELS - 1):
            @pl.when(p == q)
            def _(q=q):
                rest = (q + 1) * PANEL
                upper = done[:, rest:HEAD]
                work[rest:HEAD, :] = work[rest:HEAD, :] - lax.dot_general(
                    upper, done, (((0,), (0,)), ((), ())), precision=HIGH, preferred_element_type=F32
                )
        return carry

    lax.fori_loop(0, PANELS, panel, 0)
    linv = work[:HEAD, HEAD:]
    hi, lo = split(linv)
    linv_out[:, :HEAD] = hi
    linv_out[:, HEAD : 2 * HEAD] = hi
    linv_out[:, 2 * HEAD :] = lo
    left = jnp.concatenate([hi, lo, hi], 1)
    width = 256
    pr = lax.broadcasted_iota(jnp.int32, (HEAD, width), 0)
    pc = lax.broadcasted_iota(jnp.int32, (HEAD, width), 1)

    def some_cols(c, carry):
        at = pl.multiple_of(c * width, width)
        first = tile * col_chunks * LANES + c * width
        right = cols_out[:, pl.ds(at, width)]
        ids = pc + first
        cross = taper_cov(down, right, members_n)
        cross = cross + jnp.where(pr == ids, carry, 0.0)
        hi, lo = split(cross)
        f = jnp.dot(left, jnp.concatenate([hi, hi, lo], 0), preferred_element_type=F32)
        f = jnp.where(ids >= lax.div(pr, PANEL) * PANEL, f, 0.0)
        hi, lo = split(f)
        fcols_out[:HEAD, pl.ds(at, width)] = hi
        fcols_out[HEAD : 2 * HEAD, pl.ds(at, width)] = lo
        fcols_out[2 * HEAD :, pl.ds(at, width)] = hi
        return carry

    noise_down = jnp.sum(jnp.where(same, obs_head[...], 0.0), axis=1, keepdims=True)
    lax.fori_loop(0, cols_out.shape[1] // width, some_cols, jnp.broadcast_to(noise_down, (HEAD, width)))


def final_kernel(place_ref, rows, cols, head, linv, fcols, obs_head, obs, trailing, factor, keep):
    members_n = ROWS - 8
    step = pl.program_id(0)
    grp, tile = place_ref[0], place_ref[1]
    height = rows.shape[0]
    steps = pl.num_programs(0)
    col_span = cols.shape[1]
    first_row = (grp * steps + step) * height
    first_col = tile * col_span
    left = rows[...]
    rid = lax.broadcasted_iota(jnp.int32, (height, HEAD), 0) + first_row
    cid = lax.broadcasted_iota(jnp.int32, (height, HEAD), 1)
    cross = taper_cov(left, head[...], members_n) + jnp.where(rid == cid, obs_head[...], 0.0)
    hi, lo = split(cross)
    f = lax.dot_general(
        jnp.concatenate([hi, lo, hi], 1), linv[...], (((1,), (1,)), ((), ())), preferred_element_type=F32
    )
    f = jnp.where(rid >= lax.div(cid, PANEL) * PANEL, f, 0.0)
    keep[pl.ds(pl.multiple_of(step * height, height), height), :] = f
    hi, lo = split(f)
    f3 = jnp.concatenate([hi, hi, lo], 1)
    width = min(512, col_span)
    for c in range(0, col_span, width):
        part = cols[:, c : c + width]
        value = taper_cov(left, part, members_n)
        trailing[:, c : c + width] = value - jnp.dot(
            f3, fcols[:, c : c + width], preferred_element_type=F32
        )

    @pl.when((first_row < first_col + col_span) & (first_col < first_row + height))
    def _():
        for c in range(0, col_span, width):
            rid = lax.broadcasted_iota(jnp.int32, (height, width), 0) + first_row
            cid = lax.broadcasted_iota(jnp.int32, (height, width), 1) + (first_col + c)
            trailing[:, c : c + width] = trailing[:, c : c + width] + jnp.where(
                rid == cid, obs[:, c : c + width], 0.0
            )

    @pl.when(step == steps - 1)
    def _():
        share = factor.shape[0]
        factor[...] = keep[pl.ds(pl.multiple_of(tile * share, share), share), :]


def spec(space=pltpu.VMEM):
    return pl.BlockSpec(memory_space=space)


def per_device(
    members, courant, turb_energy, dissipation, sensor_cells, sensor_frac, sensor_count, obs_var
):
    grp_size = lax.axis_size("grp")
    tile_size = lax.axis_size("tile")
    grp = lax.axis_index("grp")
    tile = lax.axis_index("tile")
    members_n = members.shape[0]
    slots = sensor_cells.shape[1]
    blocks = grp_size * tile_size
    place = jnp.stack([grp, tile, jnp.int32(grp_size - 1), jnp.int32(tile_size - 1)]).astype(jnp.int32)

    diffusion = diffuse_rate * turb_energy * turb_energy / dissipation

    def cut(xs, ys):
        return jnp.concatenate([members[:, xs, ys], courant[:, xs, ys], diffusion[None, xs, ys]], 0)

    every = slice(None)
    x_first, x_last = cut(slice(0, 2), every), cut(slice(6, 8), every)
    y_first = jnp.swapaxes(cut(every, slice(0, 2)), 1, 2)
    y_last = jnp.swapaxes(cut(every, slice(6, 8)), 1, 2)

    def move(value, dg, dt):
        pairs = []
        for g in range(grp_size):
            for t in range(tile_size):
                if 0 <= g + dg < grp_size and 0 <= t + dt < tile_size:
                    pairs.append((g * tile_size + t, (g + dg) * tile_size + t + dt))
        return lax.ppermute(value, ("grp", "tile"), pairs)

    xlo, xhi = move(x_last, 1, 0), move(x_first, -1, 0)
    ylo, yhi = move(y_last, 0, 1), move(y_first, 0, -1)
    c_ll, c_lh = move(cut(7, 7), 1, 1), move(cut(7, 0), 1, -1)
    c_hl, c_hh = move(cut(0, 7), -1, 1), move(cut(0, 0), -1, -1)

    obs_at = jnp.minimum(grp * slots, obs_var.shape[0] - slots)
    obs_part = lax.dynamic_slice_in_dim(obs_var, obs_at, slots, 0)[None]

    message = pl.pallas_call(
        forecast_kernel,
        out_shape=jax.ShapeDtypeStruct((ROWS, slots), F32),
        in_specs=[spec(pltpu.SMEM)] * 2 + [spec()] * 17,
        out_specs=spec(),
        scratch_shapes=[pltpu.VMEM((12, 7, 8, LANES), F32), pltpu.VMEM((members_n, 64, LANES), F32)],
        compiler_params=pltpu.CompilerParams(vmem_limit_bytes=VMEM_LIMIT),
        name="forecast",
    )(
        place, sensor_count, members, courant, turb_energy, dissipation, xlo, xhi, ylo, yhi,
        y_first, y_last, c_ll, c_lh, c_hl, c_hh, sensor_cells, sensor_frac, obs_part,
    )

    everything = lax.all_gather(message, ("grp", "tile"), axis=0)
    counts = everything[:, members_n + 3, 0].astype(jnp.int32)
    offsets = jnp.cumsum(counts) - counts
    holders = -(-HEAD // slots)
    obs_head = everything[: holders * tile_size : tile_size, members_n + 4].reshape(1, -1)[:, :HEAD]

    row_span = NS // grp_size
    col_span = NS // tile_size
    rows, cols, head, linv, fcols = pl.pallas_call(
        head_kernel,
        out_shape=[
            jax.ShapeDtypeStruct((row_span, LANES), F32),
            jax.ShapeDtypeStruct((ROWS, col_span), F32),
            jax.ShapeDtypeStruct((ROWS, HEAD), F32),
            jax.ShapeDtypeStruct((HEAD, 3 * HEAD), BF16),
            jax.ShapeDtypeStruct((3 * HEAD, col_span), BF16),
        ],
        in_specs=[spec(pltpu.SMEM)] * 2 + [spec()] * 2,
        out_specs=[spec()] * 5,
        scratch_shapes=[
            pltpu.VMEM((NS // LANES + slots // LANES + 1, ROWS, LANES), F32),
            pltpu.VMEM((HEAD + PANEL, 2 * HEAD), F32),
        ],
        compiler_params=pltpu.CompilerParams(vmem_limit_bytes=VMEM_LIMIT),
        name="head",
    )(offsets, place, everything, obs_head)

    height = 256
    share = row_span // tile_size
    whole = lambda shape: pl.BlockSpec(shape, lambda i: (0, 0))
    trailing, factor = pl.pallas_call(
        final_kernel,
        grid=(row_span // height,),
        out_shape=[
            jax.ShapeDtypeStruct((row_span, col_span), F32),
            jax.ShapeDtypeStruct((share, HEAD), F32),
        ],
        in_specs=[
            spec(pltpu.SMEM),
            pl.BlockSpec((height, LANES), lambda i: (i, 0)),
            whole((ROWS, col_span)),
            whole((ROWS, HEAD)),
            whole((HEAD, 3 * HEAD)),
            whole((3 * HEAD, col_span)),
            whole((1, HEAD)),
            whole((1, col_span)),
        ],
        out_specs=[pl.BlockSpec((height, col_span), lambda i: (i, 0)), whole((share, HEAD))],
        scratch_shapes=[pltpu.VMEM((row_span, HEAD), F32)],
        compiler_params=pltpu.CompilerParams(vmem_limit_bytes=VMEM_LIMIT),
        name="final",
    )(place, rows, cols, head, linv, fcols, obs_head, obs_var[None])
    return trailing, factor


def solution(mesh):
    return jax.shard_map(
        per_device,
        mesh=mesh,
        in_specs=(
            P(None, "grp", "tile", None),
            P(None, "grp", "tile", None),
            P("grp", "tile", None),
            P("grp", "tile", None),
            P(None, ("grp", "tile")),
            P(None, ("grp", "tile")),
            P(("grp", "tile")),
            P("tile"),
        ),
        out_specs=(P("grp", "tile"), P(("grp", "tile"), None)),
        check_vma=False,
    )
```

```python
import functools
import math

import jax
import jax.numpy as jnp
from jax import lax
from jax.experimental import pallas as pl
from jax.experimental.pallas import tpu as pltpu
from jax.sharding import PartitionSpec as P

NS = 16384
PANEL = 128
PANELS = 4
SWEEPS = 2
LOC = 8
HEAD = PANEL * PANELS
ROWS = 40
LANES = 128

diffuse_rate = 0.06

HIGH = lax.Precision.HIGHEST
F32 = jnp.float32
BF16 = jnp.bfloat16
VMEM_LIMIT = 56 * 1024 * 1024


def split(value):
    hi = value.astype(BF16)
    lo = (value - hi.astype(F32)).astype(BF16)
    return hi, lo


def cut_kernel(
    mem, cour, turb, diss, x_first, x_last, y_first, y_last, diff
):
    members_n = mem.shape[0]
    t = turb[...]
    diff[0] = diffuse_rate * t * t / diss[...]

    def one(ref, i, f):
        x_first[f, 0] = ref[i, 0:8, :]
        x_first[f, 1] = ref[i, 8:16, :]
        x_last[f, 0] = ref[i, 48:56, :]
        x_last[f, 1] = ref[i, 56:64, :]
        for k in range(2):
            y_first[f, k] = ref[i, pl.ds(k, 8, stride=8), :]
            y_last[f, k] = ref[i, pl.ds(6 + k, 8, stride=8), :]

    def members_loop(i, carry):
        one(mem, i, i)
        return carry

    lax.fori_loop(0, members_n, members_loop, 0)
    for d in range(3):
        one(cour, d, members_n + d)
    one(diff, 0, members_n + 3)


def edge_kernel(xlo, xhi, last, first):
    fields = xlo.shape[0]

    def one(f, carry):
        last[pl.ds(f, 1), :] = xlo[f, 1, 7:8, :]
        last[pl.ds(fields + f, 1), :] = xhi[f, 0, 7:8, :]
        first[pl.ds(f, 1), :] = xlo[f, 1, 0:1, :]
        first[pl.ds(fields + f, 1), :] = xhi[f, 0, 0:1, :]
        return carry

    lax.fori_loop(0, fields, one, 0, unroll=4)


def forecast_kernel(
    place_ref, count_ref, mem, cour, turb, diss, xlo, xhi, ylo, yhi, own_lo, own_hi,
    edge_lo, edge_hi, cells, frac, obs, out, kc, state,
):
    members_n = mem.shape[0]
    fields = members_n + 4
    slots = cells.shape[1]
    grp, tile = place_ref[0], place_ref[1]
    last_grp, last_tile = place_ref[2], place_ref[3]
    sub = lax.broadcasted_iota(jnp.int32, (8, LANES), 0)
    lane = lax.broadcasted_iota(jnp.int32, (8, LANES), 1)

    def after(v, row):
        return jnp.where(sub == 0, jnp.broadcast_to(row, (8, LANES)), pltpu.roll(v, 1, 0))

    def before(v, row):
        return jnp.where(sub == 7, jnp.broadcast_to(row, (8, LANES)), pltpu.roll(v, 7, 0))

    def zlow(v):
        return jnp.where(lane == 0, 0.0, pltpu.roll(v, 1, 1))

    def zhigh(v):
        return jnp.where(lane == LANES - 1, 0.0, pltpu.roll(v, LANES - 1, 1))

    def diffusion(x):
        t = turb[x]
        return diffuse_rate * t * t / diss[x]

    def xplane(f, x):
        if x < 0:
            return xlo[f, x + 2]
        if x > 7:
            return xhi[f, x - 8]
        if isinstance(f, int) and f >= members_n:
            return cour[f - members_n, x] if f < members_n + 3 else diffusion(x)
        return mem[f, x]

    def row(ref, f):
        return ref[pl.ds(f, 1), :]

    def xends(f, x):
        if x < 0:
            return row(edge_lo, f), row(edge_hi, f)
        if x > 7:
            return row(edge_lo, fields + f), row(edge_hi, fields + f)
        return ylo[f, 1, x : x + 1, :], yhi[f, 0, x : x + 1, :]

    def face(cp, ep, cq, eq):
        c = 0.5 * (cp + cq)
        e = 0.5 * (ep + eq)
        return jnp.maximum(c, 0.0) + e, jnp.minimum(c, 0.0) - e

    def coefs(index, keep, depth, tangent, planes, ends):
        e_prev, e_now, e_next = planes(members_n + 3)
        e_lo, e_hi = ends(members_n + 3)
        d_prev, d_now, d_next = planes(members_n + depth)
        t_now = planes(members_n + tangent)[1]
        t_lo, t_hi = ends(members_n + tangent)
        z_now = planes(members_n + 2)[1]
        pairs = [
            face(d_prev, e_prev, d_now, e_now),
            face(d_now, e_now, d_next, e_next),
            face(after(t_now, t_lo), after(e_now, e_lo), t_now, e_now),
            face(t_now, e_now, before(t_now, t_hi), before(e_now, e_hi)),
            face(zlow(z_now), zlow(e_now), z_now, e_now),
            face(z_now, e_now, zhigh(z_now), zhigh(e_now)),
        ]
        middle = jnp.ones((8, LANES), F32)
        for axis in range(3):
            (a_lo, b_lo), (a_hi, b_hi) = pairs[2 * axis], pairs[2 * axis + 1]
            middle = middle - (a_hi - b_lo)
            kc[index, 1 + 2 * axis] = keep * a_lo
            kc[index, 2 + 2 * axis] = -(keep * b_hi)
        kc[index, 0] = keep * middle

    def kept(flag):
        return jnp.where(flag, 1.0, 0.0).astype(F32)

    for x in range(-1, 9):
        keep = 1.0
        if x < 0:
            keep = kept(grp > 0)
        if x > 7:
            keep = kept(grp < last_grp)
        coefs(
            x + 1, keep, 0, 1,
            lambda f, x=x: tuple(xplane(f, x + s) for s in (-1, 0, 1)),
            lambda f, x=x: xends(f, x),
        )

    def yplanes_lo(f):
        return ylo[f, 0], ylo[f, 1], own_lo[f, 0]

    def yplanes_hi(f):
        return own_hi[f, 1], yhi[f, 0], yhi[f, 1]

    def yends_lo(f):
        return row(edge_lo, f), row(edge_lo, fields + f)

    def yends_hi(f):
        return row(edge_hi, f), row(edge_hi, fields + f)

    coefs(10, kept(tile > 0), 1, 0, yplanes_lo, yends_lo)
    coefs(11, kept(tile < last_tile), 1, 0, yplanes_hi, yends_hi)

    def update(index, v_prev, v, v_next, r_lo, r_hi):
        return (
            kc[index, 0] * v
            + kc[index, 1] * v_prev
            + kc[index, 2] * v_next
            + kc[index, 3] * after(v, r_lo)
            + kc[index, 4] * before(v, r_hi)
            + kc[index, 5] * zlow(v)
            + kc[index, 6] * zhigh(v)
        )

    def one_member(m, total):
        planes = [xplane(m, x) for x in range(-2, 10)]
        new = [
            update(x + 1, planes[x + 1], planes[x + 2], planes[x + 3], *xends(m, x))
            for x in range(-1, 9)
        ]
        new_lo = update(10, *yplanes_lo(m), *yends_lo(m))
        new_hi = update(11, *yplanes_hi(m), *yends_hi(m))
        sums = []
        for x in range(8):
            v = update(
                x + 1, new[x], new[x + 1], new[x + 2], new_lo[x : x + 1, :], new_hi[x : x + 1, :]
            )
            state[m, x * 8 : (x + 1) * 8, :] = v
            sums.append(total[x] + v)
        return tuple(sums)

    zero = jnp.zeros((8, LANES), F32)
    total = lax.fori_loop(0, members_n, one_member, (zero,) * 8, unroll=4)
    mean = jnp.concatenate(total, 0) * (1.0 / members_n)

    base = cells[0:1, :]
    z0 = lax.rem(base, LANES)
    xy0 = lax.div(base, LANES)
    y0 = lax.rem(xy0, 8)
    x0 = lax.div(xy0, 8)
    fx, fy, fz = frac[0:1, :], frac[1:2, :], frac[2:3, :]

    def hat(size, at, f):
        iota = lax.broadcasted_iota(jnp.int32, (size, slots), 0)
        return jnp.where(iota == at, 1.0 - f, jnp.where(iota == at + 1, f, 0.0))

    wz_hi, wz_lo = split(hat(LANES, z0, fz))
    wz = jnp.concatenate([wz_hi, wz_hi, wz_lo], 0)
    wx = hat(8, x0, fx)
    wy = hat(8, y0, fy)
    wxy = jnp.concatenate([wx[x : x + 1, :] * wy for x in range(8)], 0)

    group = 8
    parts = slots // LANES

    def some_members(step, carry):
        field = state[pl.ds(step * group, group)] - mean[None]
        hi, lo = split(field.reshape(group * 64, LANES))
        along = jnp.dot(
            jnp.concatenate([hi, lo, hi], 1), wz, preferred_element_type=F32
        ).reshape(group, 64, slots)
        picked = jnp.sum(along * wxy[None], axis=1)
        picked = picked.astype(BF16).astype(F32)
        for c in range(parts):
            out[pl.ds(pl.multiple_of(c * members_n + step * group, group), group), :] = picked[
                :, c * LANES : (c + 1) * LANES
            ]
        return carry

    lax.fori_loop(0, members_n // group, some_members, 0, unroll=True)
    extras = (
        (grp * 8 + x0).astype(F32) + fx,
        (tile * 8 + y0).astype(F32) + fy,
        z0.astype(F32) + fz,
        jnp.full((1, slots), count_ref[0], jnp.int32).astype(F32),
        obs[...],
    )
    for e, value in enumerate(extras):
        for c in range(parts):
            at = (members_n + e) * parts + c
            out[at : at + 1, :] = value[:, c * LANES : (c + 1) * LANES]
    used = (members_n + len(extras)) * parts
    if used < out.shape[0]:
        out[used:, :] = jnp.zeros((out.shape[0] - used, LANES), F32)


def taper_cov(left, right, members_n):
    cov = jnp.dot(
        left[:, :members_n].astype(BF16), right[:members_n].astype(BF16), preferred_element_type=F32
    )
    dist = members_n - 1.0
    for d in range(3):
        at = members_n + d
        gap = left[:, at : at + 1] - right[at : at + 1, :]
        dist = dist + gap * gap
    return cov * pl.reciprocal(dist, approx=True)


def eliminate(a):
    groups = len(a)
    sub = lax.broadcasted_iota(jnp.int32, (8, LANES), 0)
    lane = lax.broadcasted_iota(jnp.int32, (8, LANES), 1)
    m = [jnp.where(lane == sub + 8 * g, 1.0, 0.0).astype(F32) for g in range(groups)]
    done = []

    def down(v, j):
        return jnp.broadcast_to(v[j : j + 1, :], (8, LANES))

    def across(v, k):
        return jnp.broadcast_to(v[:, k : k + 1], (8, LANES))

    for gk in range(groups):
        k0 = 8 * gk
        col = [across(a[gk], k0 + j) for j in range(8)]
        u = [[down(col[j], i) if i >= j else None for i in range(8)] for j in range(8)]
        inv = []
        for j in range(8):
            inv.append(pl.reciprocal(u[j][j], approx=True))
            for i in range(j + 1, 8):
                f = u[j][i] * inv[j]
                for k in range(i, 8):
                    u[i][k] = u[i][k] - f * u[j][k]
        ra, rm = a[gk], m[gk]
        rows_a, rows_m = [], []
        diag = u[0][0]
        for j in range(8):
            diag = jnp.where(sub == j, u[j][j], diag)
            row_a, row_m = down(ra, j), down(rm, j)
            rows_a.append(row_a)
            rows_m.append(row_m)
            if j == 7:
                break
            f = jnp.where(sub > j, col[j] * inv[j], 0.0)
            for i in range(j + 1, 8):
                col[i] = col[i] - f * u[j][i]
            ra = ra - f * row_a
            rm = rm - f * row_m
        done.append(rm * lax.rsqrt(diag))
        for g in range(gk + 1, groups):
            c = [across(a[g], k0 + j) for j in range(8)]
            ag, mg = a[g], m[g]
            for j in range(8):
                f = c[j] * inv[j]
                for i in range(j + 1, 8):
                    c[i] = c[i] - f * u[j][i]
                ag = ag - f * rows_a[j]
                mg = mg - f * rows_m[j]
            a[g], m[g] = ag, mg
    return jnp.concatenate(done, 0)


def turned(chunk):
    return jnp.concatenate([chunk, jnp.zeros((LANES - ROWS, LANES), F32)], 0).T


def head_stage(
    place_ref, pieces, patterns, parts, cols_out, head_out, down_out, linv_out, fcols_out, obs_head, full, work,
    count_vec, count_smem, sem,
):
    col_chunks = cols_out.shape[1] // LANES
    members_n = ROWS - 8
    grp, tile = place_ref[0], place_ref[1]
    tiles = place_ref[3] + 1
    sub = lax.broadcasted_iota(jnp.int32, (8, LANES), 0)
    lane8 = lax.broadcasted_iota(jnp.int32, (8, LANES), 1)
    lane = lax.broadcasted_iota(jnp.int32, (ROWS, LANES), 1)
    blocks = sum(len(p) for p in patterns)
    unit = math.sqrt(members_n - 1.0) / LOC

    def source(pattern):
        return (grp ^ pattern[0]) * tiles + (tile ^ pattern[1])

    for r in range(-(-blocks // LANES)):
        counts = jnp.zeros((1, LANES), F32)
        for piece, pattern in zip(pieces, patterns):
            for k, one in enumerate(pattern):
                at = (members_n + 3) * parts
                here = lane8[:1] + r * LANES == source(one)
                counts = jnp.where(here, piece[k, at : at + 1, :], counts)
        count_vec[r : r + 1, :] = counts.astype(jnp.int32)
    copy = pltpu.make_async_copy(count_vec, count_smem, sem)
    copy.start()
    copy.wait()

    def add_up(b, total):
        r, c = lax.div(b, LANES), lax.rem(b, LANES)
        count = count_smem[r, c]
        count_smem[r + count_smem.shape[0] // 2, c] = total
        return total + count

    lax.fori_loop(0, blocks, add_up, jnp.int32(0))

    for piece, pattern in zip(pieces, patterns):
        for k, one in enumerate(pattern):
            src = source(one)
            r, c = lax.div(src, LANES), lax.rem(src, LANES)
            count = count_smem[r, c]
            at = count_smem[r + count_smem.shape[0] // 2, c]
            chunk = lax.div(at, LANES)
            shift = lax.rem(at, LANES)
            early = lane < shift
            last = None
            for j in range(parts + 1):
                if j < parts:
                    tail = jnp.zeros((8, LANES), F32)
                    for d in range(3):
                        e = (members_n + d) * parts + j
                        tail = jnp.where(sub == d, piece[k, e : e + 1, :] * unit, tail)
                    now = jnp.concatenate([piece[k, j * members_n : (j + 1) * members_n, :], tail], 0)
                    now = pltpu.roll(now, shift, 1)
                    moved = now if j == 0 else jnp.where(early, last, now)
                else:
                    moved = last
                live = lane < shift + count - j * LANES
                if j == 0:
                    live = live & (lane >= shift)
                last = now
                full[chunk + j] = jnp.where(live, moved, full[chunk + j])

            @pl.when((lax.rem(src, tiles) == 0) & (src * parts < tiles * PANELS))
            def _(piece=piece, k=k, src=src):
                holder = lax.div(src, tiles)
                for j in range(min(parts, PANELS)):
                    e = (members_n + 4) * parts + j
                    full[full.shape[0] - 1, pl.ds(holder * min(parts, PANELS) + j, 1), :] = piece[
                        k, e : e + 1, :
                    ]

    for j in range(PANELS):
        obs_head[:, j * LANES : (j + 1) * LANES] = full[full.shape[0] - 1, j : j + 1, :]

    for c in range(col_chunks):
        cols_out[:, c * LANES : (c + 1) * LANES] = full[tile * col_chunks + c]
    for c in range(PANELS):
        head_out[:, c * LANES : (c + 1) * LANES] = full[c]
        down_out[c * LANES : (c + 1) * LANES, :] = turned(full[c])

    head = head_out[...]
    down = down_out[...]
    rid = lax.broadcasted_iota(jnp.int32, (HEAD, HEAD), 0)
    cid = lax.broadcasted_iota(jnp.int32, (HEAD, HEAD), 1)
    same = rid == cid
    work[:HEAD, :HEAD] = taper_cov(down, head, members_n) + jnp.where(same, obs_head[...], 0.0)
    work[:HEAD, HEAD:] = jnp.where(same, 1.0, 0.0).astype(F32)

    def panel(p, carry):
        at = pl.multiple_of(p * PANEL, PANEL)
        for q in range(PANELS):
            @pl.when(p == q)
            def _(q=q):
                for g in range(16):
                    work[HEAD + 8 * g : HEAD + 8 * g + 8, :PANEL] = work[
                        q * PANEL + 8 * g : q * PANEL + 8 * g + 8, q * PANEL : (q + 1) * PANEL
                    ]
        inverse = eliminate([work[HEAD + 8 * g : HEAD + 8 * g + 8, :PANEL] for g in range(16)])
        wide = pl.ds(at, HEAD + PANEL)
        done = jnp.dot(inverse, work[pl.ds(at, PANEL), wide], precision=HIGH, preferred_element_type=F32)
        work[pl.ds(at, PANEL), wide] = done
        for q in range(PANELS - 1):
            @pl.when(p == q)
            def _(q=q):
                rest = (q + 1) * PANEL
                upper = done[:, PANEL : HEAD - q * PANEL]
                some = slice(q * PANEL, HEAD + rest)
                work[rest:HEAD, some] = work[rest:HEAD, some] - lax.dot_general(
                    upper, done, (((0,), (0,)), ((), ())), precision=HIGH, preferred_element_type=F32
                )
        return carry

    lax.fori_loop(0, PANELS, panel, 0)
    linv = work[:HEAD, HEAD:]
    hi, lo = split(linv)
    linv_out[:, :HEAD] = hi
    linv_out[:, HEAD : 2 * HEAD] = hi
    linv_out[:, 2 * HEAD :] = lo
    left = jnp.concatenate([hi, lo, hi], 1)
    width = 256
    pr = lax.broadcasted_iota(jnp.int32, (HEAD, width), 0)
    pc = lax.broadcasted_iota(jnp.int32, (HEAD, width), 1)

    def some_cols(c, carry):
        at = pl.multiple_of(c * width, width)
        first = tile * col_chunks * LANES + c * width
        right = cols_out[:, pl.ds(at, width)]
        ids = pc + first
        cross = taper_cov(down, right, members_n)
        cross = cross + jnp.where(pr == ids, carry, 0.0)
        hi, lo = split(cross)
        f = jnp.dot(left, jnp.concatenate([hi, hi, lo], 0), preferred_element_type=F32)
        f = jnp.where(ids >= lax.div(pr, PANEL) * PANEL, f, 0.0)
        hi, lo = split(f)
        fcols_out[:HEAD, pl.ds(at, width)] = hi
        fcols_out[HEAD : 2 * HEAD, pl.ds(at, width)] = lo
        fcols_out[2 * HEAD :, pl.ds(at, width)] = hi
        return carry

    noise_down = jnp.sum(jnp.where(same, obs_head[...], 0.0), axis=1, keepdims=True)
    lax.fori_loop(0, cols_out.shape[1] // width, some_cols, jnp.broadcast_to(noise_down, (HEAD, width)))


def final_kernel(place_ref, *refs, patterns, parts):
    pieces = refs[: len(patterns)]
    obs, trailing, factor = refs[len(patterns) : len(patterns) + 3]
    (
        cols, head, down, linv, fcols, obs_head, full, work, count_vec, count_smem, sem, keep, lefts, factors,
    ) = refs[len(patterns) + 3 :]
    members_n = ROWS - 8
    step = pl.program_id(0)
    grp, tile = place_ref[0], place_ref[1]
    height, col_span = trailing.shape
    steps = pl.num_programs(0)
    first_row = (grp * steps + step) * height
    first_col = tile * col_span
    chunks = height // LANES

    def prepare(at, slot):
        first = (grp * steps + at) * height
        left = jnp.concatenate([turned(full[lax.div(first, LANES) + c]) for c in range(chunks)], 0)
        lefts[slot] = left
        rid = lax.broadcasted_iota(jnp.int32, (height, HEAD), 0) + first
        cid = lax.broadcasted_iota(jnp.int32, (height, HEAD), 1)
        cross = taper_cov(left, head[...], members_n) + jnp.where(rid == cid, obs_head[...], 0.0)
        hi, lo = split(cross)
        f = lax.dot_general(
            jnp.concatenate([hi, lo, hi], 1), linv[...], (((1,), (1,)), ((), ())),
            preferred_element_type=F32,
        )
        f = jnp.where(rid >= lax.div(cid, PANEL) * PANEL, f, 0.0)
        keep[pl.ds(pl.multiple_of(at * height, height), height), :] = f
        hi, lo = split(f)
        factors[slot, :, :HEAD] = hi
        factors[slot, :, HEAD : 2 * HEAD] = hi
        factors[slot, :, 2 * HEAD :] = lo

    @pl.when(step == 0)
    def _():
        head_stage(
            place_ref, pieces, patterns, parts, cols, head, down, linv, fcols, obs_head, full, work,
            count_vec, count_smem, sem,
        )
        prepare(0, 0)

    slot = lax.rem(step, 2)
    left = lefts[slot]
    f3 = factors[slot]
    prepare(jnp.minimum(step + 1, steps - 1), 1 - slot)
    width = min(512, col_span)
    for c in range(0, col_span, width):
        value = taper_cov(left, cols[:, c : c + width], members_n)
        trailing[:, c : c + width] = value - jnp.dot(
            f3, fcols[:, c : c + width], preferred_element_type=F32
        )

    @pl.when((first_row < first_col + col_span) & (first_col < first_row + height))
    def _():
        for c in range(0, col_span, width):
            rid = lax.broadcasted_iota(jnp.int32, (height, width), 0) + first_row
            cid = lax.broadcasted_iota(jnp.int32, (height, width), 1) + (first_col + c)
            trailing[:, c : c + width] = trailing[:, c : c + width] + jnp.where(
                rid == cid, obs[:, c : c + width], 0.0
            )

    @pl.when(step == steps - 1)
    def _():
        share = factor.shape[0]
        factor[...] = keep[pl.ds(pl.multiple_of(tile * share, share), share), :]


def gather(unit, grp_size, tile_size):
    def swap(piece, dg, dt):
        value, pattern = piece
        pairs = [
            (g * tile_size + t, (g ^ dg) * tile_size + (t ^ dt))
            for g in range(grp_size)
            for t in range(tile_size)
        ]
        return lax.ppermute(value, ("grp", "tile"), pairs), [(p ^ dg, q ^ dt) for p, q in pattern]

    def join(*some):
        return jnp.concatenate([v for v, _ in some], 0), sum([p for _, p in some], [])

    a = (unit[None], [(0, 0)])
    if (grp_size, tile_size) == (4, 8):
        b, c, d = swap(a, 0, 2), swap(a, 0, 4), swap(a, 0, 6)
        a = join(a, swap(a, 0, 1))
        ya = swap(a, 2, 0)
        b = join(b, swap(b, 2, 0))
        xb = swap(b, 0, 1)
        c = join(c, swap(c, 0, 1))
        yc = swap(c, 2, 0)
        d = join(d, swap(d, 2, 0))
        xd = swap(d, 0, 1)
        pieces = [a, b, ya, xb, c, d, yc, xd]
        pieces = pieces + [swap(p, 1, 0) for p in pieces]
    else:
        bit = 1
        while bit < tile_size:
            a = join(a, swap(a, 0, bit))
            bit *= 2
        bit = 1
        while bit < grp_size:
            a = join(a, swap(a, bit, 0))
            bit *= 2
        pieces = [a]
    return [v for v, _ in pieces], [p for _, p in pieces]


def spec(space=pltpu.VMEM):
    return pl.BlockSpec(memory_space=space)


def per_device(
    members, courant, turb_energy, dissipation, sensor_cells, sensor_frac, sensor_count, obs_var
):
    grp_size = lax.axis_size("grp")
    tile_size = lax.axis_size("tile")
    grp = lax.axis_index("grp")
    tile = lax.axis_index("tile")
    members_n = members.shape[0]
    slots = sensor_cells.shape[1]
    blocks = grp_size * tile_size
    place = jnp.stack([grp, tile, jnp.int32(grp_size - 1), jnp.int32(tile_size - 1)]).astype(jnp.int32)

    face = jax.ShapeDtypeStruct((members_n + 4, 2, 8, LANES), F32)
    x_first, x_last, y_first, y_last = pl.pallas_call(
        cut_kernel,
        out_shape=[face] * 4,
        in_specs=[spec()] * 4,
        out_specs=[spec()] * 4,
        scratch_shapes=[pltpu.VMEM((1, 64, LANES), F32)],
        name="cut",
    )(
        members.reshape(members_n, 64, LANES), courant.reshape(3, 64, LANES),
        turb_energy.reshape(64, LANES), dissipation.reshape(64, LANES),
    )

    def move(value, dg, dt):
        pairs = []
        for g in range(grp_size):
            for t in range(tile_size):
                if 0 <= g + dg < grp_size and 0 <= t + dt < tile_size:
                    pairs.append((g * tile_size + t, (g + dg) * tile_size + t + dt))
        return lax.ppermute(value, ("grp", "tile"), pairs)

    xlo, xhi = move(x_last, 1, 0), move(x_first, -1, 0)
    ylo, yhi = move(y_last, 0, 1), move(y_first, 0, -1)
    edge = jax.ShapeDtypeStruct((2 * (members_n + 4), LANES), F32)
    edge_last, edge_first = pl.pallas_call(
        edge_kernel,
        out_shape=[edge] * 2,
        in_specs=[spec()] * 2,
        out_specs=[spec()] * 2,
        name="edges",
    )(xlo, xhi)
    edge_lo, edge_hi = move(edge_last, 0, 1), move(edge_first, 0, -1)

    obs_at = jnp.minimum(grp * slots, obs_var.shape[0] - slots)
    obs_part = lax.dynamic_slice_in_dim(obs_var, obs_at, slots, 0)[None]

    parts = slots // LANES
    message = pl.pallas_call(
        forecast_kernel,
        out_shape=jax.ShapeDtypeStruct((-(-(members_n + 5) * parts // 8) * 8, LANES), F32),
        in_specs=[spec(pltpu.SMEM)] * 2 + [spec()] * 15,
        out_specs=spec(),
        scratch_shapes=[pltpu.VMEM((12, 7, 8, LANES), F32), pltpu.VMEM((members_n, 64, LANES), F32)],
        compiler_params=pltpu.CompilerParams(vmem_limit_bytes=VMEM_LIMIT),
        name="forecast",
    )(
        place, sensor_count, members, courant, turb_energy, dissipation, xlo, xhi, ylo, yhi,
        y_first, y_last, edge_lo, edge_hi, sensor_cells, sensor_frac, obs_part,
    )

    pieces, patterns = gather(message, grp_size, tile_size)

    row_span = NS // grp_size
    col_span = NS // tile_size
    count_rows = -(-grp_size * tile_size // LANES)
    height = 256
    share = row_span // tile_size
    trailing, factor = pl.pallas_call(
        functools.partial(final_kernel, patterns=patterns, parts=parts),
        grid=(row_span // height,),
        out_shape=[
            jax.ShapeDtypeStruct((row_span, col_span), F32),
            jax.ShapeDtypeStruct((share, HEAD), F32),
        ],
        in_specs=[spec(pltpu.SMEM)] + [spec()] * (len(pieces) + 1),
        out_specs=[pl.BlockSpec((height, col_span), lambda i: (i, 0)), pl.BlockSpec((share, HEAD), lambda i: (0, 0))],
        scratch_shapes=[
            pltpu.VMEM((ROWS, col_span), F32),
            pltpu.VMEM((ROWS, HEAD), F32),
            pltpu.VMEM((HEAD, LANES), F32),
            pltpu.VMEM((HEAD, 3 * HEAD), BF16),
            pltpu.VMEM((3 * HEAD, col_span), BF16),
            pltpu.VMEM((1, HEAD), F32),
            pltpu.VMEM((NS // LANES + parts + 2, ROWS, LANES), F32),
            pltpu.VMEM((HEAD + PANEL, 2 * HEAD), F32),
            pltpu.VMEM((2 * count_rows, LANES), jnp.int32),
            pltpu.SMEM((2 * count_rows, LANES), jnp.int32),
            pltpu.SemaphoreType.DMA,
            pltpu.VMEM((row_span, HEAD), F32),
            pltpu.VMEM((2, height, LANES), F32),
            pltpu.VMEM((2, height, 3 * HEAD), BF16),
        ],
        compiler_params=pltpu.CompilerParams(vmem_limit_bytes=VMEM_LIMIT),
        name="panels",
    )(place, *pieces, obs_var[None])
    return trailing, factor


def solution(mesh):
    return jax.shard_map(
        per_device,
        mesh=mesh,
        in_specs=(
            P(None, "grp", "tile", None),
            P(None, "grp", "tile", None),
            P("grp", "tile", None),
            P("grp", "tile", None),
            P(None, ("grp", "tile")),
            P(None, ("grp", "tile")),
            P(("grp", "tile")),
            P("tile"),
        ),
        out_specs=(P("grp", "tile"), P(("grp", "tile"), None)),
        check_vma=False,
    )
```

```python
import functools
import math

import jax
import jax.numpy as jnp
from jax import lax
from jax.experimental import pallas as pl
from jax.experimental.pallas import tpu as pltpu
from jax.sharding import PartitionSpec as P

NS = 16384
PANEL = 128
PANELS = 4
SWEEPS = 2
LOC = 8
HEAD = PANEL * PANELS
ROWS = 40
LANES = 128

diffuse_rate = 0.06

HIGH = lax.Precision.HIGHEST
F32 = jnp.float32
BF16 = jnp.bfloat16
VMEM_LIMIT = 56 * 1024 * 1024


def split(value):
    hi = value.astype(BF16)
    lo = (value - hi.astype(F32)).astype(BF16)
    return hi, lo


def cut_kernel(
    mem, cour, turb, diss, x_first, x_last, y_first, y_last, diff
):
    members_n = mem.shape[0]
    t = turb[...]
    diff[0] = diffuse_rate * t * t / diss[...]

    def one(ref, i, f):
        x_first[f, 0] = ref[i, 0:8, :]
        x_first[f, 1] = ref[i, 8:16, :]
        x_last[f, 0] = ref[i, 48:56, :]
        x_last[f, 1] = ref[i, 56:64, :]
        for k in range(2):
            y_first[f, k] = ref[i, pl.ds(k, 8, stride=8), :]
            y_last[f, k] = ref[i, pl.ds(6 + k, 8, stride=8), :]

    def members_loop(i, carry):
        one(mem, i, i)
        return carry

    lax.fori_loop(0, members_n, members_loop, 0)
    for d in range(3):
        one(cour, d, members_n + d)
    one(diff, 0, members_n + 3)


def edge_kernel(xlo, xhi, last, first):
    fields = xlo.shape[0]

    def one(f, carry):
        last[pl.ds(f, 1), :] = xlo[f, 1, 7:8, :]
        last[pl.ds(fields + f, 1), :] = xhi[f, 0, 7:8, :]
        first[pl.ds(f, 1), :] = xlo[f, 1, 0:1, :]
        first[pl.ds(fields + f, 1), :] = xhi[f, 0, 0:1, :]
        return carry

    lax.fori_loop(0, fields, one, 0, unroll=4)


def forecast_kernel(
    place_ref, count_ref, mem, cour, turb, diss, xlo, xhi, ylo, yhi, own_lo, own_hi,
    edge_lo, edge_hi, cells, frac, obs, out, kc, state,
):
    members_n = mem.shape[0]
    fields = members_n + 4
    slots = cells.shape[1]
    grp, tile = place_ref[0], place_ref[1]
    last_grp, last_tile = place_ref[2], place_ref[3]
    sub = lax.broadcasted_iota(jnp.int32, (8, LANES), 0)
    lane = lax.broadcasted_iota(jnp.int32, (8, LANES), 1)

    def after(v, row):
        return jnp.where(sub == 0, jnp.broadcast_to(row, (8, LANES)), pltpu.roll(v, 1, 0))

    def before(v, row):
        return jnp.where(sub == 7, jnp.broadcast_to(row, (8, LANES)), pltpu.roll(v, 7, 0))

    def zlow(v):
        return jnp.where(lane == 0, 0.0, pltpu.roll(v, 1, 1))

    def zhigh(v):
        return jnp.where(lane == LANES - 1, 0.0, pltpu.roll(v, LANES - 1, 1))

    def diffusion(x):
        t = turb[x]
        return diffuse_rate * t * t / diss[x]

    def xplane(f, x):
        if x < 0:
            return xlo[f, x + 2]
        if x > 7:
            return xhi[f, x - 8]
        if isinstance(f, int) and f >= members_n:
            return cour[f - members_n, x] if f < members_n + 3 else diffusion(x)
        return mem[f, x]

    def row(ref, f):
        return ref[pl.ds(f, 1), :]

    def xends(f, x):
        if x < 0:
            return row(edge_lo, f), row(edge_hi, f)
        if x > 7:
            return row(edge_lo, fields + f), row(edge_hi, fields + f)
        return ylo[f, 1, x : x + 1, :], yhi[f, 0, x : x + 1, :]

    def face(cp, ep, cq, eq):
        c = 0.5 * (cp + cq)
        e = 0.5 * (ep + eq)
        return jnp.maximum(c, 0.0) + e, jnp.minimum(c, 0.0) - e

    def coefs(index, keep, depth, tangent, planes, ends):
        e_prev, e_now, e_next = planes(members_n + 3)
        e_lo, e_hi = ends(members_n + 3)
        d_prev, d_now, d_next = planes(members_n + depth)
        t_now = planes(members_n + tangent)[1]
        t_lo, t_hi = ends(members_n + tangent)
        z_now = planes(members_n + 2)[1]
        pairs = [
            face(d_prev, e_prev, d_now, e_now),
            face(d_now, e_now, d_next, e_next),
            face(after(t_now, t_lo), after(e_now, e_lo), t_now, e_now),
            face(t_now, e_now, before(t_now, t_hi), before(e_now, e_hi)),
            face(zlow(z_now), zlow(e_now), z_now, e_now),
            face(z_now, e_now, zhigh(z_now), zhigh(e_now)),
        ]
        middle = jnp.ones((8, LANES), F32)
        for axis in range(3):
            (a_lo, b_lo), (a_hi, b_hi) = pairs[2 * axis], pairs[2 * axis + 1]
            middle = middle - (a_hi - b_lo)
            kc[index, 1 + 2 * axis] = keep * a_lo
            kc[index, 2 + 2 * axis] = -(keep * b_hi)
        kc[index, 0] = keep * middle

    def kept(flag):
        return jnp.where(flag, 1.0, 0.0).astype(F32)

    for x in range(-1, 9):
        keep = 1.0
        if x < 0:
            keep = kept(grp > 0)
        if x > 7:
            keep = kept(grp < last_grp)
        coefs(
            x + 1, keep, 0, 1,
            lambda f, x=x: tuple(xplane(f, x + s) for s in (-1, 0, 1)),
            lambda f, x=x: xends(f, x),
        )

    def yplanes_lo(f):
        return ylo[f, 0], ylo[f, 1], own_lo[f, 0]

    def yplanes_hi(f):
        return own_hi[f, 1], yhi[f, 0], yhi[f, 1]

    def yends_lo(f):
        return row(edge_lo, f), row(edge_lo, fields + f)

    def yends_hi(f):
        return row(edge_hi, f), row(edge_hi, fields + f)

    coefs(10, kept(tile > 0), 1, 0, yplanes_lo, yends_lo)
    coefs(11, kept(tile < last_tile), 1, 0, yplanes_hi, yends_hi)

    def update(index, v_prev, v, v_next, r_lo, r_hi):
        return (
            kc[index, 0] * v
            + kc[index, 1] * v_prev
            + kc[index, 2] * v_next
            + kc[index, 3] * after(v, r_lo)
            + kc[index, 4] * before(v, r_hi)
            + kc[index, 5] * zlow(v)
            + kc[index, 6] * zhigh(v)
        )

    def one_member(m, total):
        planes = [xplane(m, x) for x in range(-2, 10)]
        new = [
            update(x + 1, planes[x + 1], planes[x + 2], planes[x + 3], *xends(m, x))
            for x in range(-1, 9)
        ]
        new_lo = update(10, *yplanes_lo(m), *yends_lo(m))
        new_hi = update(11, *yplanes_hi(m), *yends_hi(m))
        sums = []
        for x in range(8):
            v = update(
                x + 1, new[x], new[x + 1], new[x + 2], new_lo[x : x + 1, :], new_hi[x : x + 1, :]
            )
            state[m, x * 8 : (x + 1) * 8, :] = v
            sums.append(total[x] + v)
        return tuple(sums)

    zero = jnp.zeros((8, LANES), F32)
    total = lax.fori_loop(0, members_n, one_member, (zero,) * 8, unroll=4)
    mean = jnp.concatenate(total, 0) * (1.0 / members_n)

    base = cells[0:1, :]
    z0 = lax.rem(base, LANES)
    xy0 = lax.div(base, LANES)
    y0 = lax.rem(xy0, 8)
    x0 = lax.div(xy0, 8)
    fx, fy, fz = frac[0:1, :], frac[1:2, :], frac[2:3, :]

    def hat(size, at, f):
        iota = lax.broadcasted_iota(jnp.int32, (size, slots), 0)
        return jnp.where(iota == at, 1.0 - f, jnp.where(iota == at + 1, f, 0.0))

    wz_hi, wz_lo = split(hat(LANES, z0, fz))
    wz = jnp.concatenate([wz_hi, wz_hi, wz_lo], 0)
    wx = hat(8, x0, fx)
    wy = hat(8, y0, fy)
    wxy = jnp.concatenate([wx[x : x + 1, :] * wy for x in range(8)], 0)

    group = 8
    parts = slots // LANES

    def some_members(step, carry):
        field = state[pl.ds(step * group, group)] - mean[None]
        hi, lo = split(field.reshape(group * 64, LANES))
        along = jnp.dot(
            jnp.concatenate([hi, lo, hi], 1), wz, preferred_element_type=F32
        ).reshape(group, 64, slots)
        picked = jnp.sum(along * wxy[None], axis=1)
        picked = picked.astype(BF16).astype(F32)
        for c in range(parts):
            out[pl.ds(pl.multiple_of(c * members_n + step * group, group), group), :] = picked[
                :, c * LANES : (c + 1) * LANES
            ]
        return carry

    lax.fori_loop(0, members_n // group, some_members, 0, unroll=True)
    extras = (
        (grp * 8 + x0).astype(F32) + fx,
        (tile * 8 + y0).astype(F32) + fy,
        z0.astype(F32) + fz,
        jnp.full((1, slots), count_ref[0], jnp.int32).astype(F32),
        obs[...],
    )
    for e, value in enumerate(extras):
        for c in range(parts):
            at = (members_n + e) * parts + c
            out[at : at + 1, :] = value[:, c * LANES : (c + 1) * LANES]
    used = (members_n + len(extras)) * parts
    if used < out.shape[0]:
        out[used:, :] = jnp.zeros((out.shape[0] - used, LANES), F32)


def taper_cov(left, right, members_n):
    cov = jnp.dot(
        left[:, :members_n].astype(BF16), right[:members_n].astype(BF16), preferred_element_type=F32
    )
    dist = members_n - 1.0
    for d in range(3):
        at = members_n + d
        gap = left[:, at : at + 1] - right[at : at + 1, :]
        dist = dist + gap * gap
    return cov * pl.reciprocal(dist, approx=True)


def eliminate(a, beside):
    groups = len(a)
    sub = lax.broadcasted_iota(jnp.int32, (8, LANES), 0)
    lane = lax.broadcasted_iota(jnp.int32, (8, LANES), 1)
    m = [jnp.where(lane == sub + 8 * g, 1.0, 0.0).astype(F32) for g in range(groups)]
    done = []

    def down(v, j):
        return jnp.broadcast_to(v[j : j + 1, :], (8, LANES))

    def across(v, k):
        return jnp.broadcast_to(v[:, k : k + 1], (8, LANES))

    for gk in range(groups):
        k0 = 8 * gk
        col = [across(a[gk], k0 + j) for j in range(8)]
        u = [[down(col[j], i) if i >= j else None for i in range(8)] for j in range(8)]
        inv = []
        todo = beside(gk)
        for j in range(8):
            inv.append(pl.reciprocal(u[j][j], approx=True))
            for piece in todo[j * len(todo) // 8 : (j + 1) * len(todo) // 8]:
                piece()
            for i in range(j + 1, 8):
                f = u[j][i] * inv[j]
                for k in range(i, 8):
                    u[i][k] = u[i][k] - f * u[j][k]
        ra, rm = a[gk], m[gk]
        rows_a, rows_m = [], []
        diag = u[0][0]
        for j in range(8):
            diag = jnp.where(sub == j, u[j][j], diag)
            row_a, row_m = down(ra, j), down(rm, j)
            rows_a.append(row_a)
            rows_m.append(row_m)
            if j == 7:
                break
            f = jnp.where(sub > j, col[j] * inv[j], 0.0)
            for i in range(j + 1, 8):
                col[i] = col[i] - f * u[j][i]
            ra = ra - f * row_a
            rm = rm - f * row_m
        done.append(rm * lax.rsqrt(diag))
        for g in range(gk + 1, groups):
            c = [across(a[g], k0 + j) for j in range(8)]
            ag, mg = a[g], m[g]
            for j in range(8):
                f = c[j] * inv[j]
                for i in range(j + 1, 8):
                    c[i] = c[i] - f * u[j][i]
                ag = ag - f * rows_a[j]
                mg = mg - f * rows_m[j]
            a[g], m[g] = ag, mg
    return jnp.concatenate(done, 0)


def turned(chunk):
    return jnp.concatenate([chunk, jnp.zeros((LANES - ROWS, LANES), F32)], 0).T


def head_stage(
    place_ref, pieces, patterns, parts, cols_out, head_out, down_out, linv_a, linv_b, fcols_out, obs_head, full,
    work, count_vec, count_smem, sem, lefts, rows_cross, cols_cross, obs_down,
):
    col_chunks = cols_out.shape[1] // LANES
    members_n = ROWS - 8
    grp, tile = place_ref[0], place_ref[1]
    tiles = place_ref[3] + 1
    sub = lax.broadcasted_iota(jnp.int32, (8, LANES), 0)
    lane8 = lax.broadcasted_iota(jnp.int32, (8, LANES), 1)
    lane = lax.broadcasted_iota(jnp.int32, (ROWS, LANES), 1)
    blocks = sum(len(p) for p in patterns)
    unit = math.sqrt(members_n - 1.0) / LOC

    def source(pattern):
        return (grp ^ pattern[0]) * tiles + (tile ^ pattern[1])

    for r in range(-(-blocks // LANES)):
        counts = jnp.zeros((1, LANES), F32)
        for piece, pattern in zip(pieces, patterns):
            for k, one in enumerate(pattern):
                at = (members_n + 3) * parts
                here = lane8[:1] + r * LANES == source(one)
                counts = jnp.where(here, piece[k, at : at + 1, :], counts)
        count_vec[r : r + 1, :] = counts.astype(jnp.int32)
    copy = pltpu.make_async_copy(count_vec, count_smem, sem)
    copy.start()
    copy.wait()

    def add_up(b, total):
        r, c = lax.div(b, LANES), lax.rem(b, LANES)
        count = count_smem[r, c]
        count_smem[r + count_smem.shape[0] // 2, c] = total
        return total + count

    lax.fori_loop(0, blocks, add_up, jnp.int32(0))

    for piece, pattern in zip(pieces, patterns):
        for k, one in enumerate(pattern):
            src = source(one)
            r, c = lax.div(src, LANES), lax.rem(src, LANES)
            count = count_smem[r, c]
            at = count_smem[r + count_smem.shape[0] // 2, c]
            chunk = lax.div(at, LANES)
            shift = lax.rem(at, LANES)
            early = lane < shift
            last = None
            for j in range(parts + 1):
                if j < parts:
                    tail = jnp.zeros((8, LANES), F32)
                    for d in range(3):
                        e = (members_n + d) * parts + j
                        tail = jnp.where(sub == d, piece[k, e : e + 1, :] * unit, tail)
                    now = jnp.concatenate([piece[k, j * members_n : (j + 1) * members_n, :], tail], 0)
                    now = pltpu.roll(now, shift, 1)
                    moved = now if j == 0 else jnp.where(early, last, now)
                else:
                    moved = last
                live = lane < shift + count - j * LANES
                if j == 0:
                    live = live & (lane >= shift)
                last = now
                full[chunk + j] = jnp.where(live, moved, full[chunk + j])

            @pl.when((lax.rem(src, tiles) == 0) & (src * parts < tiles * PANELS))
            def _(piece=piece, k=k, src=src):
                holder = lax.div(src, tiles)
                for j in range(min(parts, PANELS)):
                    e = (members_n + 4) * parts + j
                    full[full.shape[0] - 1, pl.ds(holder * min(parts, PANELS) + j, 1), :] = piece[
                        k, e : e + 1, :
                    ]

    for j in range(PANELS):
        obs_head[:, j * LANES : (j + 1) * LANES] = full[full.shape[0] - 1, j : j + 1, :]

    for c in range(col_chunks):
        cols_out[:, c * LANES : (c + 1) * LANES] = full[tile * col_chunks + c]
    for c in range(PANELS):
        head_out[:, c * LANES : (c + 1) * LANES] = full[c]
        down_out[c * LANES : (c + 1) * LANES, :] = turned(full[c])

    head = head_out[...]
    down = down_out[...]
    rid = lax.broadcasted_iota(jnp.int32, (HEAD, HEAD), 0)
    cid = lax.broadcasted_iota(jnp.int32, (HEAD, HEAD), 1)
    same = rid == cid
    noise = jnp.sum(jnp.where(same, obs_head[...], 0.0), axis=1, keepdims=True)
    obs_down[...] = jnp.broadcast_to(noise, obs_down.shape)
    span = lefts.shape[0]
    col_span = cols_out.shape[1]
    some = span // (PANELS * 16)
    per_chunk = LANES // some
    row_iota = lax.broadcasted_iota(jnp.int32, (16, HEAD), 0)
    head_iota = lax.broadcasted_iota(jnp.int32, (16, HEAD), 1)
    down_iota = lax.broadcasted_iota(jnp.int32, (8, HEAD), 0)
    col_iota = lax.broadcasted_iota(jnp.int32, (8, HEAD), 1)
    work[:HEAD, :HEAD] = taper_cov(down, head, members_n) + jnp.where(same, obs_head[...], 0.0)
    work[:HEAD, HEAD:] = jnp.where(same, 1.0, 0.0).astype(F32)

    def panel(p, carry):
        at = pl.multiple_of(p * PANEL, PANEL)
        for q in range(PANELS):
            @pl.when(p == q)
            def _(q=q):
                for g in range(16):
                    work[HEAD + 8 * g : HEAD + 8 * g + 8, :PANEL] = work[
                        q * PANEL + 8 * g : q * PANEL + 8 * g + 8, q * PANEL : (q + 1) * PANEL
                    ]
        def beside(g):
            part = p * 16 + g
            if g % per_chunk == 0:
                c = lax.div(part, per_chunk)
                lefts[pl.ds(pl.multiple_of(c * LANES, LANES), LANES), :] = turned(
                    full[grp * (span // LANES) + c]
                )
            def some_rows(r):
                at = pl.multiple_of(part * some + r, 16)
                cross = taper_cov(lefts[pl.ds(at, 16), :], head_out[...], members_n)
                same = row_iota + (grp * span + at) == head_iota
                hi, lo = split(cross + jnp.where(same, obs_head[...], 0.0))
                rows_cross[pl.ds(at, 16), :HEAD] = hi
                rows_cross[pl.ds(at, 16), HEAD:] = lo

            def some_lanes(c):
                at = pl.multiple_of(part * 8, 8)
                cross = taper_cov(down_out[pl.ds(at, 8), :], cols_out[:, c : c + HEAD], members_n)
                same = down_iota + at == col_iota + (tile * col_span + c)
                cols_cross[pl.ds(at, 8), c : c + HEAD] = cross + jnp.where(
                    same, obs_down[pl.ds(at, 8), :1], 0.0
                )

            return [functools.partial(some_rows, r) for r in range(0, some, 16)] + [
                functools.partial(some_lanes, c) for c in range(0, col_span, HEAD)
            ]

        inverse = eliminate([work[HEAD + 8 * g : HEAD + 8 * g + 8, :PANEL] for g in range(16)], beside)
        wide = pl.ds(at, HEAD + PANEL)
        done = jnp.dot(inverse, work[pl.ds(at, PANEL), wide], precision=HIGH, preferred_element_type=F32)
        work[pl.ds(at, PANEL), wide] = done
        for q in range(PANELS - 1):
            @pl.when(p == q)
            def _(q=q):
                rest = (q + 1) * PANEL
                upper = done[:, PANEL : HEAD - q * PANEL]
                some = slice(q * PANEL, HEAD + rest)
                work[rest:HEAD, some] = work[rest:HEAD, some] - lax.dot_general(
                    upper, done, (((0,), (0,)), ((), ())), precision=HIGH, preferred_element_type=F32
                )
        return carry

    lax.fori_loop(0, PANELS, panel, 0)
    half = HEAD // 2
    for out, rows, depth in ((linv_a, slice(0, half), half), (linv_b, slice(half, HEAD), HEAD)):
        hi, lo = split(work[rows, HEAD : HEAD + depth])
        out[:, :depth] = hi
        out[:, depth : 2 * depth] = hi
        out[:, 2 * depth :] = lo
    width = min(512, col_span)
    pr = lax.broadcasted_iota(jnp.int32, (half, width), 0)
    pc = lax.broadcasted_iota(jnp.int32, (half, width), 1)

    def some_cols(c, carry):
        at = pl.multiple_of(c * width, width)
        hi, lo = split(cols_cross[:, pl.ds(at, width)])
        for out, first, depth in ((linv_a, 0, half), (linv_b, half, HEAD)):
            f = jnp.dot(
                out[...], jnp.concatenate([hi[:depth], lo[:depth], hi[:depth]], 0), preferred_element_type=F32
            )
            ids = pc + (tile * col_span + c * width)
            f = jnp.where(ids >= lax.div(pr + first, PANEL) * PANEL, f, 0.0)
            f_hi, f_lo = split(f)
            fcols_out[first : first + half, pl.ds(at, width)] = f_hi
            fcols_out[HEAD + first : HEAD + first + half, pl.ds(at, width)] = f_lo
            fcols_out[2 * HEAD + first : 2 * HEAD + first + half, pl.ds(at, width)] = f_hi
        return carry

    lax.fori_loop(0, col_span // width, some_cols, 0, unroll=True)


def final_kernel(place_ref, *refs, patterns, parts):
    pieces = refs[: len(patterns)]
    obs, trailing, factor = refs[len(patterns) : len(patterns) + 3]
    (
        cols, head, down, linv_a, linv_b, fcols, obs_head, full, work, count_vec, count_smem, sem, keep, lefts,
        rows_cross, cols_cross, obs_down, factors,
    ) = refs[len(patterns) + 3 :]
    members_n = ROWS - 8
    step = pl.program_id(0)
    grp, tile = place_ref[0], place_ref[1]
    height, col_span = trailing.shape
    steps = pl.num_programs(0)
    first_row = (grp * steps + step) * height
    first_col = tile * col_span
    share = factor.shape[0]
    half = HEAD // 2

    def prepare(at, slot):
        first = (grp * steps + at) * height
        here = pl.ds(pl.multiple_of(at * height, height), height)
        rid = lax.broadcasted_iota(jnp.int32, (height, half), 0) + first
        cid = lax.broadcasted_iota(jnp.int32, (height, half), 1)
        for linv, begin, depth in ((linv_a, 0, half), (linv_b, half, HEAD)):
            hi, lo = rows_cross[here, :depth], rows_cross[here, HEAD : HEAD + depth]
            f = lax.dot_general(
                jnp.concatenate([hi, lo, hi], 1), linv[...], (((1,), (1,)), ((), ())),
                preferred_element_type=F32,
            )
            f = jnp.where(rid >= lax.div(cid + begin, PANEL) * PANEL, f, 0.0)
            keep[:, begin : begin + half] = f
            hi, lo = split(f)
            factors[slot, :, begin : begin + half] = hi
            factors[slot, :, HEAD + begin : HEAD + begin + half] = hi
            factors[slot, :, 2 * HEAD + begin : 2 * HEAD + begin + half] = lo

    def share_out(at):
        start = at * height - tile * share
        if share >= height:
            @pl.when((start >= 0) & (start < share))
            def _():
                factor[pl.ds(pl.multiple_of(start, height), height), :] = keep[...]
        else:
            @pl.when((start <= 0) & (start > -height))
            def _():
                factor[...] = keep[pl.ds(pl.multiple_of(-start, share), share), :]

    @pl.when(step == 0)
    def _():
        head_stage(
            place_ref, pieces, patterns, parts, cols, head, down, linv_a, linv_b, fcols, obs_head, full, work,
            count_vec, count_smem, sem, lefts, rows_cross, cols_cross, obs_down,
        )
        prepare(0, 0)
        share_out(0)

    slot = lax.rem(step, 2)
    left = lefts[pl.ds(pl.multiple_of(step * height, height), height), :]
    f3 = factors[slot]
    following = jnp.minimum(step + 1, steps - 1)
    width = min(512, col_span)
    for c in range(0, col_span, width):
        value = taper_cov(left, cols[:, c : c + width], members_n)
        trailing[:, c : c + width] = value - jnp.dot(
            f3, fcols[:, c : c + width], preferred_element_type=F32
        )

    prepare(following, 1 - slot)

    @pl.when((first_row < first_col + col_span) & (first_col < first_row + height))
    def _():
        for c in range(0, col_span, width):
            rid = lax.broadcasted_iota(jnp.int32, (height, width), 0) + first_row
            cid = lax.broadcasted_iota(jnp.int32, (height, width), 1) + (first_col + c)
            trailing[:, c : c + width] = trailing[:, c : c + width] + jnp.where(
                rid == cid, obs[:, c : c + width], 0.0
            )

    share_out(following)


def gather(unit, grp_size, tile_size):
    def swap(piece, dg, dt):
        value, pattern = piece
        pairs = [
            (g * tile_size + t, (g ^ dg) * tile_size + (t ^ dt))
            for g in range(grp_size)
            for t in range(tile_size)
        ]
        return lax.ppermute(value, ("grp", "tile"), pairs), [(p ^ dg, q ^ dt) for p, q in pattern]

    def join(*some):
        return jnp.concatenate([v for v, _ in some], 0), sum([p for _, p in some], [])

    a = (unit[None], [(0, 0)])
    if (grp_size, tile_size) == (4, 8):
        b, c, d = swap(a, 0, 2), swap(a, 0, 4), swap(a, 0, 6)
        a = join(a, swap(a, 0, 1))
        ya = swap(a, 2, 0)
        b = join(b, swap(b, 2, 0))
        xb = swap(b, 0, 1)
        c = join(c, swap(c, 0, 1))
        yc = swap(c, 2, 0)
        d = join(d, swap(d, 2, 0))
        xd = swap(d, 0, 1)
        pieces = [a, b, ya, xb, c, d, yc, xd]
        pieces = pieces + [swap(p, 1, 0) for p in pieces]
    else:
        bit = 1
        while bit < tile_size:
            a = join(a, swap(a, 0, bit))
            bit *= 2
        bit = 1
        while bit < grp_size:
            a = join(a, swap(a, bit, 0))
            bit *= 2
        pieces = [a]
    return [v for v, _ in pieces], [p for _, p in pieces]


def spec(space=pltpu.VMEM):
    return pl.BlockSpec(memory_space=space)


def per_device(
    members, courant, turb_energy, dissipation, sensor_cells, sensor_frac, sensor_count, obs_var
):
    grp_size = lax.axis_size("grp")
    tile_size = lax.axis_size("tile")
    grp = lax.axis_index("grp")
    tile = lax.axis_index("tile")
    members_n = members.shape[0]
    slots = sensor_cells.shape[1]
    blocks = grp_size * tile_size
    place = jnp.stack([grp, tile, jnp.int32(grp_size - 1), jnp.int32(tile_size - 1)]).astype(jnp.int32)

    face = jax.ShapeDtypeStruct((members_n + 4, 2, 8, LANES), F32)
    x_first, x_last, y_first, y_last = pl.pallas_call(
        cut_kernel,
        out_shape=[face] * 4,
        in_specs=[spec()] * 4,
        out_specs=[spec()] * 4,
        scratch_shapes=[pltpu.VMEM((1, 64, LANES), F32)],
        name="cut",
    )(
        members.reshape(members_n, 64, LANES), courant.reshape(3, 64, LANES),
        turb_energy.reshape(64, LANES), dissipation.reshape(64, LANES),
    )

    def move(value, dg, dt):
        pairs = []
        for g in range(grp_size):
            for t in range(tile_size):
                if 0 <= g + dg < grp_size and 0 <= t + dt < tile_size:
                    pairs.append((g * tile_size + t, (g + dg) * tile_size + t + dt))
        return lax.ppermute(value, ("grp", "tile"), pairs)

    xlo, xhi = move(x_last, 1, 0), move(x_first, -1, 0)
    ylo, yhi = move(y_last, 0, 1), move(y_first, 0, -1)
    edge = jax.ShapeDtypeStruct((2 * (members_n + 4), LANES), F32)
    edge_last, edge_first = pl.pallas_call(
        edge_kernel,
        out_shape=[edge] * 2,
        in_specs=[spec()] * 2,
        out_specs=[spec()] * 2,
        name="edges",
    )(xlo, xhi)
    edge_lo, edge_hi = move(edge_last, 0, 1), move(edge_first, 0, -1)

    obs_at = jnp.minimum(grp * slots, obs_var.shape[0] - slots)
    obs_part = lax.dynamic_slice_in_dim(obs_var, obs_at, slots, 0)[None]

    parts = slots // LANES
    message = pl.pallas_call(
        forecast_kernel,
        out_shape=jax.ShapeDtypeStruct((-(-(members_n + 5) * parts // 8) * 8, LANES), F32),
        in_specs=[spec(pltpu.SMEM)] * 2 + [spec()] * 15,
        out_specs=spec(),
        scratch_shapes=[pltpu.VMEM((12, 7, 8, LANES), F32), pltpu.VMEM((members_n, 64, LANES), F32)],
        compiler_params=pltpu.CompilerParams(vmem_limit_bytes=VMEM_LIMIT),
        name="forecast",
    )(
        place, sensor_count, members, courant, turb_energy, dissipation, xlo, xhi, ylo, yhi,
        y_first, y_last, edge_lo, edge_hi, sensor_cells, sensor_frac, obs_part,
    )

    pieces, patterns = gather(message, grp_size, tile_size)

    row_span = NS // grp_size
    col_span = NS // tile_size
    count_rows = -(-grp_size * tile_size // LANES)
    height = 256
    share = row_span // tile_size
    trailing, factor = pl.pallas_call(
        functools.partial(final_kernel, patterns=patterns, parts=parts),
        grid=(row_span // height,),
        out_shape=[
            jax.ShapeDtypeStruct((row_span, col_span), F32),
            jax.ShapeDtypeStruct((share, HEAD), F32),
        ],
        in_specs=[spec(pltpu.SMEM)] + [spec()] * (len(pieces) + 1),
        out_specs=[pl.BlockSpec((height, col_span), lambda i: (i, 0)), pl.BlockSpec((share, HEAD), lambda i: (0, 0))],
        scratch_shapes=[
            pltpu.VMEM((ROWS, col_span), F32),
            pltpu.VMEM((ROWS, HEAD), F32),
            pltpu.VMEM((HEAD, LANES), F32),
            pltpu.VMEM((HEAD // 2, 3 * HEAD // 2), BF16),
            pltpu.VMEM((HEAD // 2, 3 * HEAD), BF16),
            pltpu.VMEM((3 * HEAD, col_span), BF16),
            pltpu.VMEM((1, HEAD), F32),
            pltpu.VMEM((NS // LANES + parts + 2, ROWS, LANES), F32),
            pltpu.VMEM((HEAD + PANEL, 2 * HEAD), F32),
            pltpu.VMEM((2 * count_rows, LANES), jnp.int32),
            pltpu.SMEM((2 * count_rows, LANES), jnp.int32),
            pltpu.SemaphoreType.DMA,
            pltpu.VMEM((height, HEAD), F32),
            pltpu.VMEM((row_span, LANES), F32),
            pltpu.VMEM((row_span, 2 * HEAD), BF16),
            pltpu.VMEM((HEAD, col_span), F32),
            pltpu.VMEM((HEAD, LANES), F32),
            pltpu.VMEM((2, height, 3 * HEAD), BF16),
        ],
        compiler_params=pltpu.CompilerParams(vmem_limit_bytes=VMEM_LIMIT),
        name="panels",
    )(place, *pieces, obs_var[None])
    return trailing, factor


def solution(mesh):
    return jax.shard_map(
        per_device,
        mesh=mesh,
        in_specs=(
            P(None, "grp", "tile", None),
            P(None, "grp", "tile", None),
            P("grp", "tile", None),
            P("grp", "tile", None),
            P(None, ("grp", "tile")),
            P(None, ("grp", "tile")),
            P(("grp", "tile")),
            P("tile"),
        ),
        out_specs=(P("grp", "tile"), P(("grp", "tile"), None)),
        check_vma=False,
    )
```

```python
import functools
import math

import jax
import jax.numpy as jnp
from jax import lax
from jax.experimental import pallas as pl
from jax.experimental.pallas import tpu as pltpu
from jax.sharding import PartitionSpec as P

NS = 16384
PANEL = 128
PANELS = 4
SWEEPS = 2
LOC = 8
HEAD = PANEL * PANELS
ROWS = 40
DEPTH = 80
LANES = 128

diffuse_rate = 0.06

HIGH = lax.Precision.HIGHEST
F32 = jnp.float32
BF16 = jnp.bfloat16
VMEM_LIMIT = 56 * 1024 * 1024


def split(value):
    hi = value.astype(BF16)
    lo = (value - hi.astype(F32)).astype(BF16)
    return hi, lo


def cut_kernel(
    mem, cour, turb, diss, x_first, x_last, y_first, y_last, diff
):
    members_n = mem.shape[0]
    t = turb[...]
    diff[0] = diffuse_rate * t * t / diss[...]

    def one(ref, i, f):
        x_first[f, 0] = ref[i, 0:8, :]
        x_first[f, 1] = ref[i, 8:16, :]
        x_last[f, 0] = ref[i, 48:56, :]
        x_last[f, 1] = ref[i, 56:64, :]
        for k in range(2):
            y_first[f, k] = ref[i, pl.ds(k, 8, stride=8), :]
            y_last[f, k] = ref[i, pl.ds(6 + k, 8, stride=8), :]

    def members_loop(i, carry):
        one(mem, i, i)
        return carry

    lax.fori_loop(0, members_n, members_loop, 0, unroll=4)
    for d in range(3):
        one(cour, d, members_n + d)
    one(diff, 0, members_n + 3)


def edge_kernel(xlo, xhi, last, first):
    fields = xlo.shape[0]

    def one(f, carry):
        last[pl.ds(f, 1), :] = xlo[f, 1, 7:8, :]
        last[pl.ds(fields + f, 1), :] = xhi[f, 0, 7:8, :]
        first[pl.ds(f, 1), :] = xlo[f, 1, 0:1, :]
        first[pl.ds(fields + f, 1), :] = xhi[f, 0, 0:1, :]
        return carry

    lax.fori_loop(0, fields, one, 0, unroll=4)


def forecast_kernel(
    place_ref, count_ref, mem, cour, turb, diss, xlo, xhi, ylo, yhi, own_lo, own_hi,
    edge_lo, edge_hi, cells, frac, obs, out, kc, state,
):
    members_n = mem.shape[0]
    fields = members_n + 4
    slots = cells.shape[1]
    grp, tile = place_ref[0], place_ref[1]
    last_grp, last_tile = place_ref[2], place_ref[3]
    sub = lax.broadcasted_iota(jnp.int32, (8, LANES), 0)
    lane = lax.broadcasted_iota(jnp.int32, (8, LANES), 1)

    def after(v, row):
        return jnp.where(sub == 0, jnp.broadcast_to(row, (8, LANES)), pltpu.roll(v, 1, 0))

    def before(v, row):
        return jnp.where(sub == 7, jnp.broadcast_to(row, (8, LANES)), pltpu.roll(v, 7, 0))

    def zlow(v):
        return jnp.where(lane == 0, 0.0, pltpu.roll(v, 1, 1))

    def zhigh(v):
        return jnp.where(lane == LANES - 1, 0.0, pltpu.roll(v, LANES - 1, 1))

    def diffusion(x):
        t = turb[x]
        return diffuse_rate * t * t / diss[x]

    def xplane(f, x):
        if x < 0:
            return xlo[f, x + 2]
        if x > 7:
            return xhi[f, x - 8]
        if isinstance(f, int) and f >= members_n:
            return cour[f - members_n, x] if f < members_n + 3 else diffusion(x)
        return mem[f, x]

    def row(ref, f):
        return ref[pl.ds(f, 1), :]

    def xends(f, x):
        if x < 0:
            return row(edge_lo, f), row(edge_hi, f)
        if x > 7:
            return row(edge_lo, fields + f), row(edge_hi, fields + f)
        return ylo[f, 1, x : x + 1, :], yhi[f, 0, x : x + 1, :]

    def face(cp, ep, cq, eq):
        c = 0.5 * (cp + cq)
        e = 0.5 * (ep + eq)
        return jnp.maximum(c, 0.0) + e, jnp.minimum(c, 0.0) - e

    def coefs(index, keep, depth, tangent, planes, ends):
        e_prev, e_now, e_next = planes(members_n + 3)
        e_lo, e_hi = ends(members_n + 3)
        d_prev, d_now, d_next = planes(members_n + depth)
        t_now = planes(members_n + tangent)[1]
        t_lo, t_hi = ends(members_n + tangent)
        z_now = planes(members_n + 2)[1]
        pairs = [
            face(d_prev, e_prev, d_now, e_now),
            face(d_now, e_now, d_next, e_next),
            face(after(t_now, t_lo), after(e_now, e_lo), t_now, e_now),
            face(t_now, e_now, before(t_now, t_hi), before(e_now, e_hi)),
            face(zlow(z_now), zlow(e_now), z_now, e_now),
            face(z_now, e_now, zhigh(z_now), zhigh(e_now)),
        ]
        middle = jnp.ones((8, LANES), F32)
        for axis in range(3):
            (a_lo, b_lo), (a_hi, b_hi) = pairs[2 * axis], pairs[2 * axis + 1]
            middle = middle - (a_hi - b_lo)
            kc[index, 1 + 2 * axis] = keep * a_lo
            kc[index, 2 + 2 * axis] = -(keep * b_hi)
        kc[index, 0] = keep * middle

    def kept(flag):
        return jnp.where(flag, 1.0, 0.0).astype(F32)

    for x in range(-1, 9):
        keep = 1.0
        if x < 0:
            keep = kept(grp > 0)
        if x > 7:
            keep = kept(grp < last_grp)
        coefs(
            x + 1, keep, 0, 1,
            lambda f, x=x: tuple(xplane(f, x + s) for s in (-1, 0, 1)),
            lambda f, x=x: xends(f, x),
        )

    def yplanes_lo(f):
        return ylo[f, 0], ylo[f, 1], own_lo[f, 0]

    def yplanes_hi(f):
        return own_hi[f, 1], yhi[f, 0], yhi[f, 1]

    def yends_lo(f):
        return row(edge_lo, f), row(edge_lo, fields + f)

    def yends_hi(f):
        return row(edge_hi, f), row(edge_hi, fields + f)

    coefs(10, kept(tile > 0), 1, 0, yplanes_lo, yends_lo)
    coefs(11, kept(tile < last_tile), 1, 0, yplanes_hi, yends_hi)

    def update(index, v_prev, v, v_next, r_lo, r_hi):
        return (
            kc[index, 0] * v
            + kc[index, 1] * v_prev
            + kc[index, 2] * v_next
            + kc[index, 3] * after(v, r_lo)
            + kc[index, 4] * before(v, r_hi)
            + kc[index, 5] * zlow(v)
            + kc[index, 6] * zhigh(v)
        )

    def one_member(m, total):
        planes = [xplane(m, x) for x in range(-2, 10)]
        new = [
            update(x + 1, planes[x + 1], planes[x + 2], planes[x + 3], *xends(m, x))
            for x in range(-1, 9)
        ]
        new_lo = update(10, *yplanes_lo(m), *yends_lo(m))
        new_hi = update(11, *yplanes_hi(m), *yends_hi(m))
        sums = []
        for x in range(8):
            v = update(
                x + 1, new[x], new[x + 1], new[x + 2], new_lo[x : x + 1, :], new_hi[x : x + 1, :]
            )
            state[m, x * 8 : (x + 1) * 8, :] = v
            sums.append(total[x] + v)
        return tuple(sums)

    zero = jnp.zeros((8, LANES), F32)
    total = lax.fori_loop(0, members_n, one_member, (zero,) * 8, unroll=4)
    mean = jnp.concatenate(total, 0) * (1.0 / members_n)

    base = cells[0:1, :]
    z0 = lax.rem(base, LANES)
    xy0 = lax.div(base, LANES)
    y0 = lax.rem(xy0, 8)
    x0 = lax.div(xy0, 8)
    fx, fy, fz = frac[0:1, :], frac[1:2, :], frac[2:3, :]

    def hat(size, at, f):
        iota = lax.broadcasted_iota(jnp.int32, (size, slots), 0)
        return jnp.where(iota == at, 1.0 - f, jnp.where(iota == at + 1, f, 0.0))

    wz_hi, wz_lo = split(hat(LANES, z0, fz))
    wz = jnp.concatenate([wz_hi, wz_hi, wz_lo], 0)
    wx = hat(8, x0, fx)
    wy = hat(8, y0, fy)
    wxy = jnp.concatenate([wx[x : x + 1, :] * wy for x in range(8)], 0)

    group = 8
    parts = slots // LANES

    def some_members(step, carry):
        field = state[pl.ds(step * group, group)] - mean[None]
        hi, lo = split(field.reshape(group * 64, LANES))
        along = jnp.dot(
            jnp.concatenate([hi, lo, hi], 1), wz, preferred_element_type=F32
        ).reshape(group, 64, slots)
        picked = jnp.sum(along * wxy[None], axis=1)
        picked = picked.astype(BF16).astype(F32)
        for c in range(parts):
            out[pl.ds(pl.multiple_of(c * members_n + step * group, group), group), :] = picked[
                :, c * LANES : (c + 1) * LANES
            ]
        return carry

    lax.fori_loop(0, members_n // group, some_members, 0, unroll=True)
    extras = (
        (grp * 8 + x0).astype(F32) + fx,
        (tile * 8 + y0).astype(F32) + fy,
        z0.astype(F32) + fz,
        jnp.full((1, slots), count_ref[0], jnp.int32).astype(F32),
        obs[...],
    )
    for e, value in enumerate(extras):
        for c in range(parts):
            at = (members_n + e) * parts + c
            out[at : at + 1, :] = value[:, c * LANES : (c + 1) * LANES]
    used = (members_n + len(extras)) * parts
    if used < out.shape[0]:
        out[used:, :] = jnp.zeros((out.shape[0] - used, LANES), F32)


def taper_cov(left, right):
    some = left[:, :DEPTH].astype(BF16)
    cov = jnp.dot(some, right[:DEPTH], preferred_element_type=F32)
    dist = jnp.dot(some, right[DEPTH:], preferred_element_type=F32)
    return cov * pl.reciprocal(dist, approx=True)


def taper_tile(left, right, places):
    members_n = ROWS - 8
    cov = jnp.dot(left[:, :DEPTH].astype(BF16), right[:DEPTH], preferred_element_type=F32)
    dist = members_n - 1.0
    for d in range(3):
        gap = left[:, DEPTH + d : DEPTH + d + 1] - places[d : d + 1, :]
        dist = dist + gap * gap
    return cov * pl.reciprocal(dist, approx=True)


def thirds(value):
    first = value.astype(BF16).astype(F32)
    rest = value - first
    second = rest.astype(BF16).astype(F32)
    return first, second, (rest - second).astype(BF16).astype(F32)


def sides(chunk, centers):
    members_n = ROWS - 8
    sub = lax.broadcasted_iota(jnp.int32, (8, LANES), 0)
    place = jnp.where(sub == 0, centers[0], jnp.where(sub == 1, centers[1], centers[2]))
    at = jnp.where(sub < 3, chunk[members_n:] - place, 0.0)
    square = at * at
    norm = square[0:1] + square[1:2] + square[2:3]
    norm = jnp.broadcast_to(norm, (8, LANES))
    p1, p2, p3 = thirds(at)

    def rows(value):
        first, second, third = thirds(value)
        return jnp.where(sub == 3, first, jnp.where(sub == 4, second, jnp.where(sub == 5, third, 0.0)))

    ones = jnp.where((sub > 2) & (sub < 6), 1.0, 0.0)
    left = [chunk[:members_n], p1 + rows(norm), p1 + ones, p2, p2, p1, p3, at]
    q1, q2, q3 = -2.0 * p1, -2.0 * p2, -2.0 * p3
    right = [q1 + ones, q2 + rows(norm + (members_n - 1.0)), q1, q2, q3, q1]
    return jnp.concatenate(left, 0), jnp.concatenate(right, 0), at


def eliminate(a, beside):
    groups = len(a)
    sub = lax.broadcasted_iota(jnp.int32, (8, LANES), 0)
    lane = lax.broadcasted_iota(jnp.int32, (8, LANES), 1)
    m = [jnp.where(lane == sub + 8 * g, 1.0, 0.0).astype(F32) for g in range(groups)]
    done = []

    def down(v, j):
        return jnp.broadcast_to(v[j : j + 1, :], (8, LANES))

    def across(v, k):
        return jnp.broadcast_to(v[:, k : k + 1], (8, LANES))

    ahead = None
    for gk in range(groups):
        k0 = 8 * gk
        col = ahead or [across(a[gk], k0 + j) for j in range(8)]
        u = [[down(col[j], i) if i >= j else None for i in range(8)] for j in range(8)]
        inv = []
        todo = beside(gk)
        for j in range(8):
            inv.append(pl.reciprocal(u[j][j], approx=True))
            for piece in todo[j * len(todo) // 8 : (j + 1) * len(todo) // 8]:
                piece()
            for i in range(j + 1, 8):
                f = u[j][i] * inv[j]
                for k in range(i, 8):
                    u[i][k] = u[i][k] - f * u[j][k]
        ra, rm = a[gk], m[gk]
        rows_a, rows_m = [], []
        diag = u[0][0]
        for j in range(8):
            diag = jnp.where(sub == j, u[j][j], diag)
            row_a, row_m = down(ra, j), down(rm, j)
            rows_a.append(row_a)
            rows_m.append(row_m)
            if j == 7:
                break
            f = jnp.where(sub > j, col[j] * inv[j], 0.0)
            for i in range(j + 1, 8):
                col[i] = col[i] - f * u[j][i]
            ra = ra - f * row_a
            rm = rm - f * row_m
        done.append(rm * lax.rsqrt(diag))
        for g in range(gk + 1, groups):
            c = [across(a[g], k0 + j) for j in range(8)]
            ag, mg = a[g], m[g]
            if g == gk + 1:
                ahead = [across(ag, k0 + 8 + j) for j in range(8)]
            for j in range(8):
                f = c[j] * inv[j]
                for i in range(j + 1, 8):
                    c[i] = c[i] - f * u[j][i]
                if g == gk + 1:
                    for i in range(8):
                        ahead[i] = ahead[i] - f * down(c[j], i)
                ag = ag - f * rows_a[j]
                mg = mg - f * rows_m[j]
            a[g], m[g] = ag, mg
    return jnp.concatenate(done, 0)


def turned(chunk):
    return jnp.concatenate([chunk, jnp.zeros((LANES - DEPTH - 8, LANES), F32)], 0).T


def head_stage(
    place_ref, pieces, patterns, parts, cols_out, col_places, head_out, down_out, linv_a, linv_b, fcols_out, obs_head, full,
    work, count_vec, count_smem, sem, lefts, rows_cross, cols_cross, obs_down,
):
    col_chunks = cols_out.shape[1] // LANES
    members_n = ROWS - 8
    grp, tile = place_ref[0], place_ref[1]
    tiles = place_ref[3] + 1
    sub = lax.broadcasted_iota(jnp.int32, (8, LANES), 0)
    lane8 = lax.broadcasted_iota(jnp.int32, (8, LANES), 1)
    lane = lax.broadcasted_iota(jnp.int32, (ROWS, LANES), 1)
    blocks = sum(len(p) for p in patterns)
    unit = math.sqrt(members_n - 1.0) / LOC

    def source(pattern):
        return (grp ^ pattern[0]) * tiles + (tile ^ pattern[1])

    for r in range(-(-blocks // LANES)):
        counts = jnp.zeros((1, LANES), F32)
        for piece, pattern in zip(pieces, patterns):
            for k, one in enumerate(pattern):
                at = (members_n + 3) * parts
                here = lane8[:1] + r * LANES == source(one)
                counts = jnp.where(here, piece[k, at : at + 1, :], counts)
        count_vec[r : r + 1, :] = counts.astype(jnp.int32)
    copy = pltpu.make_async_copy(count_vec, count_smem, sem)
    copy.start()
    copy.wait()

    def add_up(b, total):
        r, c = lax.div(b, LANES), lax.rem(b, LANES)
        count = count_smem[r, c]
        count_smem[r + count_smem.shape[0] // 2, c] = total
        return total + count

    lax.fori_loop(0, blocks, add_up, jnp.int32(0))

    for piece, pattern in zip(pieces, patterns):
        for k, one in enumerate(pattern):
            src = source(one)
            r, c = lax.div(src, LANES), lax.rem(src, LANES)
            count = count_smem[r, c]
            at = count_smem[r + count_smem.shape[0] // 2, c]
            chunk = lax.div(at, LANES)
            shift = lax.rem(at, LANES)
            early = lane < shift
            last = None
            for j in range(parts + 1):
                if j < parts:
                    tail = jnp.zeros((8, LANES), F32)
                    for d in range(3):
                        e = (members_n + d) * parts + j
                        tail = jnp.where(sub == d, piece[k, e : e + 1, :] * unit, tail)
                    now = jnp.concatenate([piece[k, j * members_n : (j + 1) * members_n, :], tail], 0)
                    now = pltpu.roll(now, shift, 1)
                    moved = now if j == 0 else jnp.where(early, last, now)
                else:
                    moved = last
                live = lane < shift + count - j * LANES
                if j == 0:
                    live = live & (lane >= shift)
                last = now
                full[chunk + j] = jnp.where(live, moved, full[chunk + j])

            @pl.when((lax.rem(src, tiles) == 0) & (src * parts < tiles * PANELS))
            def _(piece=piece, k=k, src=src):
                holder = lax.div(src, tiles)
                for j in range(min(parts, PANELS)):
                    e = (members_n + 4) * parts + j
                    full[full.shape[0] - 1, pl.ds(holder * min(parts, PANELS) + j, 1), :] = piece[
                        k, e : e + 1, :
                    ]

    for j in range(PANELS):
        obs_head[:, j * LANES : (j + 1) * LANES] = full[full.shape[0] - 1, j : j + 1, :]

    centers = [
        (place_ref[2] + 1).astype(F32) * (4.0 * unit), tiles.astype(F32) * (4.0 * unit), LANES * 0.5 * unit
    ]

    def across_side(out, places, c, chunk):
        lanes = pl.ds(pl.multiple_of(c * LANES, LANES), LANES)
        _, right, at = sides(chunk, centers)
        right = right.astype(BF16)
        if places is not None:
            places[:, lanes] = at
        out[:members_n, lanes] = chunk[:members_n].astype(BF16)
        out[members_n : DEPTH + members_n, lanes] = jnp.zeros((DEPTH, LANES), BF16)
        out[DEPTH + members_n :, lanes] = right

    def across_cols(c, carry):
        across_side(cols_out, col_places, c, full[tile * col_chunks + c])
        return carry

    lax.fori_loop(0, col_chunks, across_cols, 0, unroll=4)
    for c in range(PANELS):
        across_side(head_out, None, c, full[c])
        down_out[c * LANES : (c + 1) * LANES, :] = turned(sides(full[c], centers)[0])

    head = head_out[...]
    down = down_out[...]
    rid = lax.broadcasted_iota(jnp.int32, (HEAD, HEAD), 0)
    cid = lax.broadcasted_iota(jnp.int32, (HEAD, HEAD), 1)
    same = rid == cid
    noise = jnp.sum(jnp.where(same, obs_head[...], 0.0), axis=1, keepdims=True)
    obs_down[...] = jnp.broadcast_to(noise, obs_down.shape)
    span = lefts.shape[0]
    col_span = cols_out.shape[1]
    some = span // (PANELS * 16)
    per_chunk = LANES // some
    row_iota = lax.broadcasted_iota(jnp.int32, (16, HEAD), 0)
    head_iota = lax.broadcasted_iota(jnp.int32, (16, HEAD), 1)
    down_iota = lax.broadcasted_iota(jnp.int32, (8, HEAD), 0)
    col_iota = lax.broadcasted_iota(jnp.int32, (8, HEAD), 1)
    work[:HEAD, :HEAD] = taper_cov(down, head) + jnp.where(same, obs_head[...], 0.0)
    work[:HEAD, HEAD:] = jnp.where(same, 1.0, 0.0).astype(F32)

    def panel(p, carry):
        at = pl.multiple_of(p * PANEL, PANEL)
        for q in range(PANELS):
            @pl.when(p == q)
            def _(q=q):
                for g in range(16):
                    work[HEAD + 8 * g : HEAD + 8 * g + 8, :PANEL] = work[
                        q * PANEL + 8 * g : q * PANEL + 8 * g + 8, q * PANEL : (q + 1) * PANEL
                    ]
        def beside(g):
            part = p * 16 + g
            if g % per_chunk == 0:
                c = lax.div(part, per_chunk)
                lefts[pl.ds(pl.multiple_of(c * LANES, LANES), LANES), :] = turned(
                    sides(full[grp * (span // LANES) + c], centers)[0]
                )
            def some_rows(r):
                at = pl.multiple_of(part * some + r, 16)
                cross = taper_cov(lefts[pl.ds(at, 16), :], head_out[...])
                same = row_iota + (grp * span + at) == head_iota
                hi, lo = split(cross + jnp.where(same, obs_head[...], 0.0))
                rows_cross[pl.ds(at, 16), :HEAD] = hi
                rows_cross[pl.ds(at, 16), HEAD:] = lo

            def some_lanes(c):
                at = pl.multiple_of(part * 8, 8)
                cross = taper_cov(down_out[pl.ds(at, 8), :], cols_out[:, c : c + HEAD])
                same = down_iota + at == col_iota + (tile * col_span + c)
                cols_cross[pl.ds(at, 8), c : c + HEAD] = cross + jnp.where(
                    same, obs_down[pl.ds(at, 8), :1], 0.0
                )

            return [functools.partial(some_rows, r) for r in range(0, some, 16)] + [
                functools.partial(some_lanes, c) for c in range(0, col_span, HEAD)
            ]

        inverse = eliminate([work[HEAD + 8 * g : HEAD + 8 * g + 8, :PANEL] for g in range(16)], beside)
        wide = pl.ds(at, HEAD + PANEL)
        done = jnp.dot(inverse, work[pl.ds(at, PANEL), wide], precision=HIGH, preferred_element_type=F32)
        work[pl.ds(at, PANEL), wide] = done
        for q in range(PANELS - 1):
            @pl.when(p == q)
            def _(q=q):
                rest = (q + 1) * PANEL
                upper = done[:, PANEL : HEAD - q * PANEL]
                some = slice(q * PANEL, HEAD + rest)
                work[rest:HEAD, some] = work[rest:HEAD, some] - lax.dot_general(
                    upper, done, (((0,), (0,)), ((), ())), precision=HIGH, preferred_element_type=F32
                )
        return carry

    lax.fori_loop(0, PANELS, panel, 0)
    half = HEAD // 2
    for out, rows, depth in ((linv_a, slice(0, half), half), (linv_b, slice(half, HEAD), HEAD)):
        hi, lo = split(work[rows, HEAD : HEAD + depth])
        out[:, :depth] = hi
        out[:, depth : 2 * depth] = hi
        out[:, 2 * depth :] = lo
    width = min(512, col_span)
    pr = lax.broadcasted_iota(jnp.int32, (half, width), 0)
    pc = lax.broadcasted_iota(jnp.int32, (half, width), 1)

    def some_cols(c, carry):
        at = pl.multiple_of(c * width, width)
        hi, lo = split(cols_cross[:, pl.ds(at, width)])
        for out, first, depth in ((linv_a, 0, half), (linv_b, half, HEAD)):
            f = jnp.dot(
                out[...], jnp.concatenate([hi[:depth], lo[:depth], hi[:depth]], 0), preferred_element_type=F32
            )
            ids = pc + (tile * col_span + c * width)
            f = jnp.where(ids >= lax.div(pr + first, PANEL) * PANEL, f, 0.0)
            f_hi, f_lo = split(f)
            fcols_out[first : first + half, pl.ds(at, width)] = f_hi
            fcols_out[HEAD + first : HEAD + first + half, pl.ds(at, width)] = f_lo
            fcols_out[2 * HEAD + first : 2 * HEAD + first + half, pl.ds(at, width)] = f_hi
        return carry

    lax.fori_loop(0, col_span // width, some_cols, 0, unroll=True)


def final_kernel(place_ref, *refs, patterns, parts):
    pieces = refs[: len(patterns)]
    obs, trailing, factor = refs[len(patterns) : len(patterns) + 3]
    (
        cols, col_places, head, down, linv_a, linv_b, fcols, obs_head, full, work, count_vec, count_smem, sem, keep, lefts,
        rows_cross, cols_cross, obs_down, factors,
    ) = refs[len(patterns) + 3 :]
    members_n = ROWS - 8
    step = pl.program_id(0)
    grp, tile = place_ref[0], place_ref[1]
    height, col_span = trailing.shape
    steps = pl.num_programs(0)
    first_row = (grp * steps + step) * height
    first_col = tile * col_span
    share = factor.shape[0]
    half = HEAD // 2

    def prepare(at, slot):
        first = (grp * steps + at) * height
        here = pl.ds(pl.multiple_of(at * height, height), height)
        rid = lax.broadcasted_iota(jnp.int32, (height, half), 0) + first
        cid = lax.broadcasted_iota(jnp.int32, (height, half), 1)
        for linv, begin, depth in ((linv_a, 0, half), (linv_b, half, HEAD)):
            hi, lo = rows_cross[here, :depth], rows_cross[here, HEAD : HEAD + depth]
            f = lax.dot_general(
                jnp.concatenate([hi, lo, hi], 1), linv[...], (((1,), (1,)), ((), ())),
                preferred_element_type=F32,
            )
            f = jnp.where(rid >= lax.div(cid + begin, PANEL) * PANEL, f, 0.0)
            keep[:, begin : begin + half] = f
            hi, lo = split(f)
            factors[slot, :, begin : begin + half] = hi
            factors[slot, :, HEAD + begin : HEAD + begin + half] = hi
            factors[slot, :, 2 * HEAD + begin : 2 * HEAD + begin + half] = lo

    def share_out(at):
        start = at * height - tile * share
        if share >= height:
            @pl.when((start >= 0) & (start < share))
            def _():
                factor[pl.ds(pl.multiple_of(start, height), height), :] = keep[...]
        else:
            @pl.when((start <= 0) & (start > -height))
            def _():
                factor[...] = keep[pl.ds(pl.multiple_of(-start, share), share), :]

    @pl.when(step == 0)
    def _():
        head_stage(
            place_ref, pieces, patterns, parts, cols, col_places, head, down, linv_a, linv_b, fcols, obs_head, full, work,
            count_vec, count_smem, sem, lefts, rows_cross, cols_cross, obs_down,
        )
        prepare(0, 0)
        share_out(0)

    slot = lax.rem(step, 2)
    left = lefts[pl.ds(pl.multiple_of(step * height, height), height), :]
    f3 = factors[slot]
    following = jnp.minimum(step + 1, steps - 1)
    width = min(512, col_span)
    for c in range(0, col_span, width):
        value = taper_tile(left, cols[:, c : c + width], col_places[:, c : c + width])
        trailing[:, c : c + width] = value - jnp.dot(
            f3, fcols[:, c : c + width], preferred_element_type=F32
        )

    prepare(following, 1 - slot)

    @pl.when((first_row < first_col + col_span) & (first_col < first_row + height))
    def _():
        for c in range(0, col_span, width):
            rid = lax.broadcasted_iota(jnp.int32, (height, width), 0) + first_row
            cid = lax.broadcasted_iota(jnp.int32, (height, width), 1) + (first_col + c)
            trailing[:, c : c + width] = trailing[:, c : c + width] + jnp.where(
                rid == cid, obs[:, c : c + width], 0.0
            )

    share_out(following)


def gather(unit, grp_size, tile_size):
    def swap(piece, dg, dt):
        value, pattern = piece
        pairs = [
            (g * tile_size + t, (g ^ dg) * tile_size + (t ^ dt))
            for g in range(grp_size)
            for t in range(tile_size)
        ]
        return lax.ppermute(value, ("grp", "tile"), pairs), [(p ^ dg, q ^ dt) for p, q in pattern]

    def join(*some):
        return jnp.concatenate([v for v, _ in some], 0), sum([p for _, p in some], [])

    a = (unit[None], [(0, 0)])
    if (grp_size, tile_size) == (4, 8):
        b, c, d = swap(a, 0, 2), swap(a, 0, 4), swap(a, 0, 6)
        a = join(a, swap(a, 0, 1))
        ya = swap(a, 2, 0)
        b = join(b, swap(b, 2, 0))
        xb = swap(b, 0, 1)
        c = join(c, swap(c, 0, 1))
        yc = swap(c, 2, 0)
        d = join(d, swap(d, 2, 0))
        xd = swap(d, 0, 1)
        pieces = [a, b, ya, xb, c, d, yc, xd]
        pieces = pieces + [swap(p, 1, 0) for p in pieces]
    else:
        bit = 1
        while bit < tile_size:
            a = join(a, swap(a, 0, bit))
            bit *= 2
        bit = 1
        while bit < grp_size:
            a = join(a, swap(a, bit, 0))
            bit *= 2
        pieces = [a]
    return [v for v, _ in pieces], [p for _, p in pieces]


def spec(space=pltpu.VMEM):
    return pl.BlockSpec(memory_space=space)


def per_device(
    members, courant, turb_energy, dissipation, sensor_cells, sensor_frac, sensor_count, obs_var
):
    grp_size = lax.axis_size("grp")
    tile_size = lax.axis_size("tile")
    grp = lax.axis_index("grp")
    tile = lax.axis_index("tile")
    members_n = members.shape[0]
    slots = sensor_cells.shape[1]
    blocks = grp_size * tile_size
    place = jnp.stack([grp, tile, jnp.int32(grp_size - 1), jnp.int32(tile_size - 1)]).astype(jnp.int32)

    face = jax.ShapeDtypeStruct((members_n + 4, 2, 8, LANES), F32)
    x_first, x_last, y_first, y_last = pl.pallas_call(
        cut_kernel,
        out_shape=[face] * 4,
        in_specs=[spec()] * 4,
        out_specs=[spec()] * 4,
        scratch_shapes=[pltpu.VMEM((1, 64, LANES), F32)],
        name="cut",
    )(
        members.reshape(members_n, 64, LANES), courant.reshape(3, 64, LANES),
        turb_energy.reshape(64, LANES), dissipation.reshape(64, LANES),
    )

    def move(value, dg, dt):
        pairs = []
        for g in range(grp_size):
            for t in range(tile_size):
                if 0 <= g + dg < grp_size and 0 <= t + dt < tile_size:
                    pairs.append((g * tile_size + t, (g + dg) * tile_size + t + dt))
        return lax.ppermute(value, ("grp", "tile"), pairs)

    xlo, xhi = move(x_last, 1, 0), move(x_first, -1, 0)
    ylo, yhi = move(y_last, 0, 1), move(y_first, 0, -1)
    edge = jax.ShapeDtypeStruct((2 * (members_n + 4), LANES), F32)
    edge_last, edge_first = pl.pallas_call(
        edge_kernel,
        out_shape=[edge] * 2,
        in_specs=[spec()] * 2,
        out_specs=[spec()] * 2,
        name="edges",
    )(xlo, xhi)
    edge_lo, edge_hi = move(edge_last, 0, 1), move(edge_first, 0, -1)

    obs_at = jnp.minimum(grp * slots, obs_var.shape[0] - slots)
    obs_part = lax.dynamic_slice_in_dim(obs_var, obs_at, slots, 0)[None]

    parts = slots // LANES
    message = pl.pallas_call(
        forecast_kernel,
        out_shape=jax.ShapeDtypeStruct((-(-(members_n + 5) * parts // 8) * 8, LANES), F32),
        in_specs=[spec(pltpu.SMEM)] * 2 + [spec()] * 15,
        out_specs=spec(),
        scratch_shapes=[pltpu.VMEM((12, 7, 8, LANES), F32), pltpu.VMEM((members_n, 64, LANES), F32)],
        compiler_params=pltpu.CompilerParams(vmem_limit_bytes=VMEM_LIMIT),
        name="forecast",
    )(
        place, sensor_count, members, courant, turb_energy, dissipation, xlo, xhi, ylo, yhi,
        y_first, y_last, edge_lo, edge_hi, sensor_cells, sensor_frac, obs_part,
    )

    pieces, patterns = gather(message, grp_size, tile_size)

    row_span = NS // grp_size
    col_span = NS // tile_size
    count_rows = -(-grp_size * tile_size // LANES)
    height = 256
    share = row_span // tile_size
    trailing, factor = pl.pallas_call(
        functools.partial(final_kernel, patterns=patterns, parts=parts),
        grid=(row_span // height,),
        out_shape=[
            jax.ShapeDtypeStruct((row_span, col_span), F32),
            jax.ShapeDtypeStruct((share, HEAD), F32),
        ],
        in_specs=[spec(pltpu.SMEM)] + [spec()] * (len(pieces) + 1),
        out_specs=[pl.BlockSpec((height, col_span), lambda i: (i, 0)), pl.BlockSpec((share, HEAD), lambda i: (0, 0))],
        scratch_shapes=[
            pltpu.VMEM((2 * DEPTH, col_span), BF16),
            pltpu.VMEM((8, col_span), F32),
            pltpu.VMEM((2 * DEPTH, HEAD), BF16),
            pltpu.VMEM((HEAD, LANES), F32),
            pltpu.VMEM((HEAD // 2, 3 * HEAD // 2), BF16),
            pltpu.VMEM((HEAD // 2, 3 * HEAD), BF16),
            pltpu.VMEM((3 * HEAD, col_span), BF16),
            pltpu.VMEM((1, HEAD), F32),
            pltpu.VMEM((NS // LANES + parts + 2, ROWS, LANES), F32),
            pltpu.VMEM((HEAD + PANEL, 2 * HEAD), F32),
            pltpu.VMEM((2 * count_rows, LANES), jnp.int32),
            pltpu.SMEM((2 * count_rows, LANES), jnp.int32),
            pltpu.SemaphoreType.DMA,
            pltpu.VMEM((height, HEAD), F32),
            pltpu.VMEM((row_span, LANES), F32),
            pltpu.VMEM((row_span, 2 * HEAD), BF16),
            pltpu.VMEM((HEAD, col_span), F32),
            pltpu.VMEM((HEAD, LANES), F32),
            pltpu.VMEM((2, height, 3 * HEAD), BF16),
        ],
        compiler_params=pltpu.CompilerParams(vmem_limit_bytes=VMEM_LIMIT),
        name="panels",
    )(place, *pieces, obs_var[None])
    return trailing, factor


def solution(mesh):
    return jax.shard_map(
        per_device,
        mesh=mesh,
        in_specs=(
            P(None, "grp", "tile", None),
            P(None, "grp", "tile", None),
            P("grp", "tile", None),
            P("grp", "tile", None),
            P(None, ("grp", "tile")),
            P(None, ("grp", "tile")),
            P(("grp", "tile")),
            P("tile"),
        ),
        out_specs=(P("grp", "tile"), P(("grp", "tile"), None)),
        check_vma=False,
    )
```
